1024 devices in a mesh: band: 256 (over z, y, core), lon: 4 (over x).
Axes of the slice: x: 4, y: 8, z: 16, core: 2. Of those that a mesh axis runs over, the one named last changes fastest.
Arguments:
- grid_state: bfloat16 [131072, 512], P(('band', 'lon')), may hold values from -6 to 6
- mesh_state: bfloat16 [16384, 512], P(('band', 'lon')), may hold values from -6 to 6
- edge_weights: bfloat16 [3, 3, 512, 512], replicated, may hold values from -0.25 to 0.25
- node_weights: bfloat16 [3, 3, 512, 512], replicated, may hold values from -0.25 to 0.25
- enc_recv: int32 [131072, 2], P(('band', 'lon')), may hold values from 0 to 16383, as said below
- proc_send: int32 [16384, 6], P(('band', 'lon')), may hold values from 0 to 16383, as said below
- long_send: int32 [1024, 6], P(('band', 'lon')), may hold values from 0 to 1023, as said below
- dec_send: int32 [131072, 3], P(('band', 'lon')), may hold values from 0 to 16383, as said below
Outputs:
- grid_out: bfloat16 [131072, 512], P(('band', 'lon'))
- mesh_two: bfloat16 [16384, 512], P(('band', 'lon'))
The draws below stay inside these ranges and needn't reach their ends.
Inputs may be any that keep to these rules, and one draw needn't show every extreme that they name: enc_recv[g, k] is a mesh node of band g // 512 or of a band beside it, the band of node m being m // 64. proc_send[m, k] is a node of band m // 64 or of a band beside it. long_send[c, j] is a coarse node of band c // 4 or of a band beside it, the band of coarse node c being c // 4. dec_send[g, k] is a mesh node of band g // 512 or of a band beside it.
All inputs are finite; a program needn't handle non-finite values.
Results may differ from the reference program's by a relative error of at most 0.019.
Values may be sent and summed in bfloat16 or wider, within the bound.
No kernel may reach another device: no remote copies, remote signals or barrier semaphores. Data moves between devices by JAX's collectives and lax.ppermute only.
A program may use at most 32 MiB of HBM per device.

```python
import jax
import jax.numpy as jnp
from jax import lax

D = 512
MESH_DEV = 16
K_ENC = 2
K_SHORT = 6
K_LONG = 6
K_DEC = 3
BANDS = 256
BAND_GRID = 512
BAND_MESH = 64
GRID = 131072
MESH = 16384
COARSE = 1024


def band_local(key, total_rows, rows_band, count, targets_band):
    first_key, second_key = jax.random.split(key)
    home = (jnp.arange(total_rows, dtype=jnp.int32) // rows_band)[:, None]
    offsets = jax.random.randint(first_key, (total_rows, count), -1, 2, dtype=jnp.int32)
    target = jnp.clip(home + offsets, 0, BANDS - 1)
    within = jax.random.randint(second_key, (total_rows, count), 0, targets_band, dtype=jnp.int32)
    return (target * targets_band + within).astype(jnp.int32)


def draw_enc_recv(key, part):
    key = jax.random.fold_in(key, 11)
    return band_local(key, GRID, BAND_GRID, K_ENC, BAND_MESH)


def draw_proc_send(key, part):
    key = jax.random.fold_in(key, 23)
    return band_local(key, MESH, BAND_MESH, K_SHORT, BAND_MESH)


def draw_long_send(key, part):
    key = jax.random.fold_in(key, 29)
    return band_local(key, COARSE, COARSE // BANDS, K_LONG, COARSE // BANDS)


def draw_dec_send(key, part):
    key = jax.random.fold_in(key, 37)
    return band_local(key, GRID, BAND_GRID, K_DEC, BAND_MESH)


def block_levels(rng, dims, cuts, smallest, largest):
    factor_of, own = 1.0, jax.random.fold_in(rng, 6)
    for dim, parts in cuts:
        steps = jnp.exp(jax.random.uniform(jax.random.fold_in(own, dim), (parts,), jnp.float32, smallest / len(cuts), largest / len(cuts)))
        factor_of = factor_of * jnp.repeat(steps, dims[dim] // parts).reshape([-1 if axis == dim else 1 for axis in range(len(dims))])
    return factor_of


def scatter_about(key, shape, deviation, bound, cuts=(), kind=jnp.bfloat16):
    drawn = deviation * jax.random.normal(key, shape, jnp.float32)
    if cuts:
        drawn = drawn * block_levels(key, shape, cuts, -0.22, 0.18)
    return jnp.clip(drawn, -bound, bound).astype(kind)


def setup_inputs(seed: int = 0) -> dict:
    splits = jax.random.split(jax.random.key(seed), 9)
    return {
        "grid_state": scatter_about(splits[0], (GRID, D), 1.0, 6.0, ((0, 1024),)),
        "mesh_state": scatter_about(splits[1], (MESH, D), 1.0, 6.0, ((0, 1024),)),
        "edge_weights": scatter_about(splits[2], (3, 3, D, D), D ** -0.5, 0.25),
        "node_weights": scatter_about(splits[3], (3, 3, D, D), D ** -0.5, 0.25),
        "enc_recv": draw_enc_recv(jax.random.fold_in(splits[8], 71), 0),
        "proc_send": draw_proc_send(jax.random.fold_in(splits[8], 71), 0),
        "long_send": draw_long_send(jax.random.fold_in(splits[8], 71), 0),
        "dec_send": draw_dec_send(jax.random.fold_in(splits[8], 71), 0),
    }


def layer_norm(values):
    average = lax.optimization_barrier(jnp.mean(values, axis=-1, keepdims=True))
    centred = values - average
    spread = lax.optimization_barrier(jnp.mean(centred * centred, axis=-1, keepdims=True))
    return centred * lax.rsqrt(spread + 1e-05)

def edge_messages(before, out_weights):
    hidden = jax.nn.silu(before).astype(jnp.bfloat16)
    shaped = hidden.reshape(-1, hidden.shape[-1])
    result = layer_norm(jnp.dot(shaped, out_weights, preferred_element_type=jnp.float32))
    return result.reshape(before.shape)

def node_update(state, aggregate, weights):
    inner = jnp.dot(state, weights[0], preferred_element_type=jnp.float32)
    inner = inner + jnp.dot(aggregate.astype(jnp.bfloat16), weights[1], preferred_element_type=jnp.float32)
    hidden = jax.nn.silu(inner).astype(jnp.bfloat16)
    outer = layer_norm(jnp.dot(hidden, weights[2], preferred_element_type=jnp.float32))
    return (state.astype(jnp.float32) + outer).astype(jnp.bfloat16)

def reference(grid_state, mesh_state, edge_weights, node_weights, enc_recv, proc_send, long_send, dec_send):
    width = grid_state.shape[1]
    band_ids = jnp.arange(BANDS, dtype=jnp.int32)
    recv_all = jnp.dot(mesh_state, edge_weights[0, 1], preferred_element_type=jnp.float32)

    def encode_band(running, band_id):
        grid_rows = lax.dynamic_slice_in_dim(grid_state, band_id * BAND_GRID, BAND_GRID, 0)
        receivers = lax.dynamic_slice_in_dim(enc_recv, band_id * BAND_GRID, BAND_GRID, 0)
        sent_proj = jnp.dot(grid_rows, edge_weights[0, 0], preferred_element_type=jnp.float32)
        messages = edge_messages(sent_proj[:, None, :] + recv_all[receivers], edge_weights[0, 2])
        running = running.at[receivers.reshape(-1)].add(messages.reshape(-1, width))
        return (running, None)
    enc_sum, _ = lax.scan(encode_band, jnp.zeros((MESH, width), jnp.float32), band_ids)
    mesh_one = node_update(mesh_state, enc_sum, node_weights[0])
    send_all = jnp.dot(mesh_one, edge_weights[1, 0], preferred_element_type=jnp.float32)
    recv_mesh = jnp.dot(mesh_one, edge_weights[1, 1], preferred_element_type=jnp.float32)

    def process_band(band_id):
        near = lax.dynamic_slice_in_dim(proc_send, band_id * BAND_MESH, BAND_MESH, 0)
        own_proj = lax.dynamic_slice_in_dim(recv_mesh, band_id * BAND_MESH, BAND_MESH, 0)
        return lax.optimization_barrier(jnp.sum(edge_messages(send_all[near] + own_proj[:, None, :], edge_weights[1, 2]), axis=1))
    proc_sum = lax.map(process_band, band_ids).reshape(MESH, width)
    coarse_rows = jnp.arange(COARSE, dtype=jnp.int32) * MESH_DEV
    far_before = send_all[long_send * MESH_DEV] + recv_mesh[coarse_rows][:, None, :]
    far_sum = lax.optimization_barrier(jnp.sum(edge_messages(far_before, edge_weights[1, 2]), axis=1))
    proc_sum = proc_sum.at[coarse_rows].add(far_sum)
    mesh_two = node_update(mesh_one, proc_sum, node_weights[1])
    send_two = jnp.dot(mesh_two, edge_weights[2, 0], preferred_element_type=jnp.float32)

    def decode_band(band_id):
        grid_rows = lax.dynamic_slice_in_dim(grid_state, band_id * BAND_GRID, BAND_GRID, 0)
        senders = lax.dynamic_slice_in_dim(dec_send, band_id * BAND_GRID, BAND_GRID, 0)
        own_proj = jnp.dot(grid_rows, edge_weights[2, 1], preferred_element_type=jnp.float32)
        return lax.optimization_barrier(jnp.sum(edge_messages(send_two[senders] + own_proj[:, None, :], edge_weights[2, 2]), axis=1))
    dec_sum = lax.map(decode_band, band_ids).reshape(GRID, width)
    grid_out = node_update(grid_state, dec_sum, node_weights[2])
    return (grid_out, mesh_two)
```

```python
import jax
import jax.numpy as jnp
from jax import lax
from jax.experimental import pallas as pl
from jax.experimental.pallas import tpu as pltpu
from jax.sharding import PartitionSpec as P

BF = jnp.bfloat16
F32 = jnp.float32
NONE = 384


def mm(a, b):
    return jnp.dot(a, b, preferred_element_type=F32)


def silu(x):
    half = 0.5 * x
    return half + half * jnp.tanh(half)


def layer_norm(values):
    average = jnp.mean(values, axis=-1, keepdims=True)
    centred = values - average
    spread = jnp.mean(centred * centred, axis=-1, keepdims=True)
    return centred * lax.rsqrt(spread + 1e-05)


def update(state, aggregate, w0, w1, w2):
    inner = mm(state, w0) + mm(aggregate.astype(BF), w1)
    outer = layer_norm(mm(silu(inner).astype(BF), w2))
    return (state.astype(F32) + outer).astype(BF)


def slot_of(target_band, band):
    step = jnp.where(band % 2 == 0, target_band - band, band - target_band)
    return jnp.where(step < 0, 2, step)


def one_hot(index, rows, dtype=BF):
    lanes = lax.broadcasted_iota(jnp.int32, (index.shape[0], rows), 1)
    return jnp.where(lanes == index, 1.0, 0.0).astype(dtype)


def pack_kernel(where_ref, grid_ref, mesh_ref, enc_ref, proc_ref, far_ref, out_ref, enc_buf, proc_buf, far_buf, rows, sems):
    small = [
        pltpu.make_async_copy(src, dst, sems.at[n])
        for n, (src, dst) in enumerate(((enc_ref, enc_buf), (proc_ref, proc_buf), (far_ref, far_buf)))
    ]
    large = []
    for d in range(4):
        large.append(pltpu.make_async_copy(grid_ref, out_ref.at[d, 0:128], sems.at[3 + d]))
        large.append(pltpu.make_async_copy(mesh_ref, out_ref.at[d, 128:144], sems.at[7 + d]))
    for copy in small + large:
        copy.start()
    band = where_ref[0]
    rows[...] = jnp.full(rows.shape, float(NONE), F32)
    for copy in small:
        copy.wait()
    enc = enc_buf[...]
    rows[0:2, :] = (slot_of(enc >> 6, band) * 64 + (enc & 63)).astype(F32)
    proc = proc_buf[...]
    rows[2:8, 0:16] = (slot_of(proc >> 6, band) * 64 + (proc & 63)).astype(F32)
    far = far_buf[...]
    rows[8:9, 0:6] = (slot_of(far >> 2, band) * 64 + (far & 3) * 16).astype(F32)
    index = rows[...].astype(BF)
    for d in range(4):
        out_ref[d, 144:160, 0:128] = index
        out_ref[d, 144:160, 128:512] = jnp.zeros((16, 384), BF)
    for copy in large:
        copy.wait()


def encode_kernel(where_ref, all_ref, pair_ref, cross_ref, ew_ref, acc_ref, p1_ref, p2_ref, up_ref, down_ref, ohs, msgs):
    own = [all_ref[l, 128:144] for l in range(4)]
    table = jnp.concatenate([*own, pair_ref[...], cross_ref[...]], axis=0)
    rows_id = lax.broadcasted_iota(jnp.int32, (192, 128), 0)
    recv = mm(table, ew_ref[0, 1]).astype(BF)
    w_send, w_out = ew_ref[0, 0], ew_ref[0, 2]
    for l in range(4):
        index = all_ref[l, 144:160, 0:128].astype(F32)
        cols = index.T.astype(jnp.int32)
        flat = index.astype(jnp.int32)
        for k in range(2):
            start = l * 256 + k * 128
            ohs[:, start : start + 128] = jnp.where(rows_id == flat[k : k + 1, :], 1.0, 0.0).astype(BF)
        hot = jnp.concatenate([one_hot(cols[:, k : k + 1], 192) for k in range(2)], axis=0)
        sent = mm(all_ref[l, 0:128], w_send)
        before = mm(hot, recv) + jnp.concatenate([sent, sent], axis=0)
        result = layer_norm(mm(silu(before).astype(BF), w_out))
        msgs[l * 256 : (l + 1) * 256] = result.astype(BF)
    total = mm(ohs[...], msgs[...])
    acc_ref[...] = total
    own, pair, cross = (total[64 * n : 64 * n + 64].astype(BF) for n in range(3))
    p1_ref[0:64] = own
    p1_ref[64:128] = pair
    p2_ref[0:64] = own
    p2_ref[64:128] = cross
    even = where_ref[0] % 2 == 0

    @pl.when(even)
    def _():
        up_ref[...] = pair
        down_ref[...] = cross

    @pl.when(jnp.logical_not(even))
    def _():
        up_ref[...] = cross
        down_ref[...] = pair


def process_kernel(
    where_ref, acc_ref, r1_ref, r2_ref, up_ref, down_ref, part_ref, pair_ref, cross_ref, ew_ref, nw_ref, band_ref, own_ref, hots
):
    near_id = lax.broadcasted_iota(jnp.int32, (16, 1), 0)
    far_id = lax.broadcasted_iota(jnp.int32, (8, 1), 0)
    lanes = lax.broadcasted_iota(jnp.int32, (16, 256), 1)
    for l in range(4):
        cols = part_ref[l, 144:160, 0:128].astype(F32).T.astype(jnp.int32)
        for k in range(6):
            hit = jnp.logical_or(lanes == cols[0:16, 2 + k : 3 + k], lanes == near_id + (192 + 16 * l))
            hots[l * 128 + 16 * k : l * 128 + 16 * k + 16] = jnp.where(hit, 1.0, 0.0).astype(BF)
        hit = jnp.logical_or(lanes == cols[0:16, 8:9], lanes == 192 + 16 * l)
        hots[l * 128 + 96 : l * 128 + 112] = jnp.where(hit, 1.0, 0.0).astype(BF)
        hots[l * 128 + 112 : l * 128 + 128] = jnp.zeros((16, 256), BF)
    table = jnp.concatenate([*[part_ref[l, 128:144] for l in range(4)], pair_ref[...], cross_ref[...]], axis=0)
    even = where_ref[0] % 2 == 0
    above, below = up_ref[...].astype(F32), down_ref[...].astype(F32)
    far_pair = jnp.where(even, below, above)
    far_cross = jnp.where(even, above, below)
    own = acc_ref[0:64] + r1_ref[64:128].astype(F32) + r2_ref[64:128].astype(F32)
    pair = acc_ref[64:128] + r1_ref[0:64].astype(F32) + far_pair
    cross = acc_ref[128:192] + r2_ref[0:64].astype(F32) + far_cross
    sums = jnp.concatenate([own, pair, cross], axis=0)
    one = update(table, sums, nw_ref[0, 0], nw_ref[0, 1], nw_ref[0, 2])
    send = mm(one, ew_ref[1, 0]).astype(BF)
    recv = mm(one[0:64], ew_ref[1, 1]).astype(BF)
    both = jnp.concatenate([send, recv], axis=0)
    w_out = ew_ref[1, 2]
    parts = []
    for l in range(0, 4, 2):
        before = mm(hots[l * 128 : (l + 2) * 128], both)
        messages = layer_norm(mm(silu(before).astype(BF), w_out))
        for m in range(2):
            base = 128 * m
            near = messages[base : base + 16]
            for k in range(1, 6):
                near = near + messages[base + 16 * k : base + 16 * k + 16]
            far = jnp.where(far_id < 6, messages[base + 96 : base + 104], 0.0)
            far = jnp.sum(far, axis=0, keepdims=True)
            parts.append(near + jnp.where(near_id == 0, far, 0.0))
    sums = jnp.concatenate(parts, axis=0)
    two = update(one[0:64], sums, nw_ref[1, 0], nw_ref[1, 1], nw_ref[1, 2])
    band_ref[...] = two
    lon = where_ref[1]
    for l in range(4):

        @pl.when(lon == l)
        def _():
            own_ref[...] = two[16 * l : 16 * l + 16]


def decode_kernel(where_ref, grid_ref, dec_ref, own_ref, pair_ref, cross_ref, ew_ref, nw_ref, out_ref, rows):
    index = dec_ref[...]
    rows[...] = jnp.zeros(rows.shape, F32)
    rows[0:3, :] = (slot_of(index >> 6, where_ref[0]) * 64 + (index & 63)).astype(F32)
    index = rows[...].T.astype(jnp.int32)
    state = grid_ref[...]
    table = jnp.concatenate([own_ref[...], pair_ref[...], cross_ref[...]], axis=0)
    send = mm(table, ew_ref[2, 0]).astype(BF)
    recv = mm(state, ew_ref[2, 1])
    w_out = ew_ref[2, 2]
    sums = None
    for k in range(3):
        before = mm(one_hot(index[:, k : k + 1], 192), send) + recv
        messages = layer_norm(mm(silu(before).astype(BF), w_out))
        sums = messages if sums is None else sums + messages
    out_ref[...] = update(state, sums, nw_ref[2, 0], nw_ref[2, 1], nw_ref[2, 2])


SMEM = pl.BlockSpec(memory_space=pltpu.SMEM)
VMEM = pl.BlockSpec(memory_space=pltpu.VMEM)
HBM = pl.BlockSpec(memory_space=pltpu.HBM)
MIB = 1024 * 1024


def params(limit=16):
    return pltpu.CompilerParams(vmem_limit_bytes=limit * MIB)


def cost(products):
    return pl.CostEstimate(flops=2 * products * 512 * 512, bytes_accessed=8 * MIB, transcendentals=0)


def per_device(
    grid_state, mesh_state, edge_weights, node_weights, enc_recv, proc_send, long_send, dec_send
):
    width = grid_state.shape[1]
    bands = lax.axis_size("band")
    where = jnp.stack([lax.axis_index("band"), lax.axis_index("lon")]).astype(jnp.int32)
    across = [(i, i + 1 if i % 2 else i - 1) for i in range(1, bands - 1)]
    within = [(i, i ^ 1) for i in range(bands)]
    upward = [(i, i + 2) for i in range(bands - 2)]
    downward = [(i + 2, i) for i in range(bands - 2)]

    def sides(pair_block, cross_block):
        cross = lax.ppermute(cross_block, "band", across)
        pair = lax.ppermute(pair_block, "band", within)
        return pair, cross

    shape = jax.ShapeDtypeStruct
    packed = pl.pallas_call(
        pack_kernel,
        in_specs=[SMEM] + [HBM] * 5,
        out_specs=VMEM,
        out_shape=shape((4, 160, width), BF),
        scratch_shapes=[
            pltpu.VMEM((2, 128), jnp.int32),
            pltpu.VMEM((6, 16), jnp.int32),
            pltpu.VMEM((1, 6), jnp.int32),
            pltpu.VMEM((16, 128), F32),
            pltpu.SemaphoreType.DMA((11,)),
        ],
        compiler_params=params(16),
        cost_estimate=cost(8000),
        name="pack",
    )(where, *(pltpu.with_memory_space_constraint(x, pltpu.HBM) for x in (grid_state, mesh_state, enc_recv.T, proc_send.T, long_send)))
    with jax.named_scope("gather_lon"):
        packed = lax.all_to_all(packed, "lon", 0, 0)
    with jax.named_scope("mesh_sides"):
        band_state = packed[:, 128:144].reshape(64, width)
        pair_state, cross_state = sides(band_state, band_state)
    acc, p1, p2, up, down = pl.pallas_call(
        encode_kernel,
        in_specs=[SMEM] + [VMEM] * 4,
        out_specs=[VMEM] * 5,
        out_shape=[
            shape((192, width), F32),
            shape((128, width), BF),
            shape((128, width), BF),
            shape((64, width), BF),
            shape((64, width), BF),
        ],
        scratch_shapes=[pltpu.VMEM((192, 1024), BF), pltpu.VMEM((1024, width), BF)],
        compiler_params=params(),
        cost_estimate=cost(8000),
        name="encode",
    )(where, packed, pair_state, cross_state, edge_weights)
    with jax.named_scope("sum_sides"):
        r_up = lax.ppermute(up, "band", upward)
        r_down = lax.ppermute(down, "band", downward)
        r1, r2 = sides(p1, p2)
    band_two, mesh_two = pl.pallas_call(
        process_kernel,
        in_specs=[SMEM] + [VMEM] * 10,
        out_specs=[VMEM, VMEM],
        out_shape=[shape((64, width), BF), shape((16, width), BF)],
        scratch_shapes=[pltpu.VMEM((512, 256), BF)],
        compiler_params=params(),
        cost_estimate=cost(8000),
        name="process",
    )(where, acc, r1, r2, r_up, r_down, packed, pair_state, cross_state, edge_weights, node_weights)
    with jax.named_scope("two_sides"):
        pair_two, cross_two = sides(band_two, band_two)
    grid_out = pl.pallas_call(
        decode_kernel,
        in_specs=[SMEM] + [VMEM] * 7,
        out_specs=VMEM,
        out_shape=shape(grid_state.shape, BF),
        scratch_shapes=[pltpu.VMEM((8, 128), F32)],
        compiler_params=params(),
        cost_estimate=cost(8000),
        name="decode",
    )(where, grid_state, dec_send.T, band_two, pair_two, cross_two, edge_weights, node_weights)
    return (grid_out, mesh_two)


def solution(mesh):
    rows = P(("band", "lon"), None)
    in_specs = (rows, rows, P(), P(), rows, rows, rows, rows)
    return jax.shard_map(
        per_device, mesh=mesh, in_specs=in_specs, out_specs=(rows, rows), check_vma=False
    )
```

```python
import jax
import jax.numpy as jnp
from jax import lax
from jax.experimental import pallas as pl
from jax.experimental.pallas import tpu as pltpu
from jax.sharding import PartitionSpec as P

BF = jnp.bfloat16
F32 = jnp.float32
NONE = 384


def mm(a, b):
    return jnp.dot(a, b, preferred_element_type=F32)


def silu(x):
    half = 0.5 * x
    return half + half * jnp.tanh(half)


def layer_norm(values):
    average = jnp.mean(values, axis=-1, keepdims=True)
    centred = values - average
    spread = jnp.mean(centred * centred, axis=-1, keepdims=True)
    return centred * lax.rsqrt(spread + 1e-05)


def update(state, inner, aggregate, w1, w2):
    inner = inner + mm(aggregate.astype(BF), w1)
    outer = layer_norm(mm(silu(inner).astype(BF), w2))
    return (state.astype(F32) + outer).astype(BF)


def slot_of(target_band, band):
    step = jnp.where(band % 2 == 0, target_band - band, band - target_band)
    return jnp.where(step < 0, 2, step)


def one_hot(index, rows, dtype=BF):
    lanes = lax.broadcasted_iota(jnp.int32, (index.shape[0], rows), 1)
    return jnp.where(lanes == index, 1.0, 0.0).astype(dtype)


def pack_kernel(grid_ref, mesh_ref, enc_ref, proc_ref, far_ref, out_ref, enc_buf, proc_buf, far_buf, rows, sems):
    small = [
        pltpu.make_async_copy(src, dst, sems.at[n])
        for n, (src, dst) in enumerate(((enc_ref, enc_buf), (proc_ref, proc_buf), (far_ref, far_buf)))
    ]
    large = []
    large.append(pltpu.make_async_copy(grid_ref, out_ref.at[0:128], sems.at[3]))
    large.append(pltpu.make_async_copy(mesh_ref, out_ref.at[128:144], sems.at[4]))
    for copy in small + large:
        copy.start()
    band = lax.axis_index("band")
    rows[...] = jnp.full(rows.shape, float(NONE), F32)
    for copy in small:
        copy.wait()
    enc = enc_buf[...]
    rows[0:2, :] = (slot_of(enc >> 6, band) * 64 + (enc & 63)).astype(F32)
    proc = proc_buf[...]
    rows[2:8, 0:16] = (slot_of(proc >> 6, band) * 64 + (proc & 63)).astype(F32)
    far = far_buf[...]
    rows[8:9, 0:6] = (slot_of(far >> 2, band) * 64 + (far & 3) * 16).astype(F32)
    index = rows[...].astype(BF)
    out_ref[176:192, 0:128] = index
    out_ref[176:192, 128:512] = jnp.zeros((16, 384), BF)
    for copy in large:
        copy.wait()


def window(all_ref):
    return jnp.concatenate(
        [all_ref[l, 128 + 16 * s : 144 + 16 * s] for s in range(3) for l in range(4)], axis=0
    )


def encode_first_kernel(all_ref, ew_ref, sent_ref, hot_ref, spread_ref):
    rows_id = lax.broadcasted_iota(jnp.int32, (192, 128), 0)
    for l in range(4):
        sent_ref[l * 128 : (l + 1) * 128] = mm(all_ref[l, 0:128], ew_ref[0, 0])
        index = all_ref[l, 176:192, 0:128].astype(F32)
        cols = index.T.astype(jnp.int32)
        flat = index.astype(jnp.int32)
        for k in range(2):
            start = l * 256 + k * 128
            spread_ref[:, start : start + 128] = jnp.where(rows_id == flat[k : k + 1, :], 1.0, 0.0).astype(BF)
            hot_ref[start : start + 128] = one_hot(cols[:, k : k + 1], 192)


def encode_kernel(all_ref, sent_ref, hot_ref, spread_ref, ew_ref, acc_ref, p1_ref, far_ref, p2_ref, msgs):
    table = window(all_ref)
    recv = mm(table, ew_ref[0, 1]).astype(BF)
    for l in range(4):
        sent = sent_ref[l * 128 : (l + 1) * 128]
        before = mm(hot_ref[l * 256 : (l + 1) * 256], recv) + jnp.concatenate([sent, sent], axis=0)
        result = layer_norm(mm(silu(before).astype(BF), ew_ref[0, 2]))
        msgs[l * 256 : (l + 1) * 256] = result.astype(BF)
    total = mm(spread_ref[...], msgs[...])
    acc_ref[...] = total
    p1_ref[...] = total[0:128].astype(BF)
    cross = total[128:192].astype(BF)
    far_ref[...] = cross
    p2_ref[0:64] = cross
    p2_ref[64:128] = cross


def process_first_kernel(all_ref, nw_ref, after_ref, inner_ref, hots):
    near_id = lax.broadcasted_iota(jnp.int32, (16, 1), 0)
    lanes = lax.broadcasted_iota(jnp.int32, (16, 256), 1)
    far = []
    for l in range(4):
        cols = all_ref[l, 176:192, 0:128].astype(F32).T.astype(jnp.int32)
        for k in range(6):
            hit = jnp.logical_or(lanes == cols[0:16, 2 + k : 3 + k], lanes == near_id + (192 + 16 * l))
            hots[l * 96 + 16 * k : l * 96 + 16 * k + 16] = jnp.where(hit, 1.0, 0.0).astype(BF)
        far.append(jnp.logical_or(lanes[0:8] == cols[0:8, 8:9], lanes[0:8] == 192 + 16 * l))
    hots[384:416] = jnp.concatenate([jnp.where(hit, 1.0, 0.0) for hit in far], axis=0).astype(BF)
    table = window(all_ref)
    inner_ref[...] = mm(table, nw_ref[0, 0])


def process_kernel(
    acc_ref, r1_ref, r2_ref, far_ref, all_ref, inner_ref, hots, ew_ref, nw_ref, after_ref, band_ref, own_ref
):
    table = window(all_ref)
    own = acc_ref[0:64] + r1_ref[64:128].astype(F32) + r2_ref[0:64].astype(F32)
    pair = acc_ref[64:128] + r1_ref[0:64].astype(F32) + far_ref[...].astype(F32)
    cross = acc_ref[128:192] + r2_ref[64:128].astype(F32)
    sums = jnp.concatenate([own, pair, cross], axis=0)
    one = update(table, inner_ref[...], sums, nw_ref[0, 1], nw_ref[0, 2])
    send = mm(one, ew_ref[1, 0]).astype(BF)
    recv = mm(one[0:64], ew_ref[1, 1]).astype(BF)
    both = jnp.concatenate([send, recv], axis=0)
    inner = mm(one[0:64], nw_ref[1, 0])
    near_id = lax.broadcasted_iota(jnp.int32, (16, 1), 0)
    far_id = lax.broadcasted_iota(jnp.int32, (8, 1), 0)
    near, far = [], []
    for start, size in ((0, 192), (192, 224)):
        before = mm(hots[start : start + size], both)
        messages = layer_norm(mm(silu(before).astype(BF), ew_ref[1, 2]))
        for m in range(2):
            total = messages[96 * m : 96 * m + 16]
            for k in range(1, 6):
                total = total + messages[96 * m + 16 * k : 96 * m + 16 * k + 16]
            near.append(total)
    for l in range(4):
        values = jnp.where(far_id < 6, messages[192 + 8 * l : 200 + 8 * l], 0.0)
        far.append(jnp.sum(values, axis=0, keepdims=True))
    parts = [a + jnp.where(near_id == 0, b, 0.0) for a, b in zip(near, far)]
    sums = jnp.concatenate(parts, axis=0)
    two = update(one[0:64], inner, sums, nw_ref[1, 1], nw_ref[1, 2])
    band_ref[...] = two
    lon = lax.axis_index("lon")
    for l in range(4):

        @pl.when(lon == l)
        def _():
            own_ref[...] = two[16 * l : 16 * l + 16]


def decode_first_kernel(grid_ref, dec_ref, ew_ref, nw_ref, after_ref, recv_ref, inner_ref, hots, rows):
    index = dec_ref[...]
    rows[...] = jnp.zeros(rows.shape, F32)
    rows[0:3, :] = (slot_of(index >> 6, lax.axis_index("band")) * 64 + (index & 63)).astype(F32)
    index = rows[...].T.astype(jnp.int32)
    for k in range(3):
        hots[k * 128 : (k + 1) * 128] = one_hot(index[:, k : k + 1], 192)
    recv_ref[...] = mm(grid_ref[...], ew_ref[2, 1])
    inner_ref[...] = mm(grid_ref[...], nw_ref[2, 0])


def decode_kernel(grid_ref, own_ref, pair_ref, cross_ref, recv_ref, inner_ref, hots, ew_ref, nw_ref, out_ref):
    table = jnp.concatenate([own_ref[...], pair_ref[...], cross_ref[...]], axis=0)
    send = mm(table, ew_ref[2, 0]).astype(BF)
    recv = recv_ref[...]
    sums = None
    for k in range(3):
        before = mm(hots[k * 128 : (k + 1) * 128], send) + recv
        messages = layer_norm(mm(silu(before).astype(BF), ew_ref[2, 2]))
        sums = messages if sums is None else sums + messages
    out_ref[...] = update(grid_ref[...], inner_ref[...], sums, nw_ref[2, 1], nw_ref[2, 2])


VMEM = pl.BlockSpec(memory_space=pltpu.VMEM)
HBM = pl.BlockSpec(memory_space=pltpu.HBM)
ANY = pl.BlockSpec(memory_space=pl.ANY)
MIB = 1024 * 1024


def kernel(body, name, operands, outs, scratch=(), limit=16, products=4000, spaces=None):
    return pl.pallas_call(
        body,
        in_specs=spaces or [VMEM] * len(operands),
        out_specs=[VMEM] * len(outs),
        out_shape=[jax.ShapeDtypeStruct(dims, kind) for dims, kind in outs],
        scratch_shapes=list(scratch),
        compiler_params=pltpu.CompilerParams(vmem_limit_bytes=limit * MIB),
        cost_estimate=pl.CostEstimate(
            flops=2 * products * 512 * 512, bytes_accessed=8 * MIB, transcendentals=0
        ),
        name=name,
    )(*operands)


def per_device(
    grid_state, mesh_state, edge_weights, node_weights, enc_recv, proc_send, long_send, dec_send
):
    width = grid_state.shape[1]
    bands = lax.axis_size("band")
    across = [(i, i + 1 if i % 2 else i - 1) for i in range(1, bands - 1)]
    within = [(i, i ^ 1) for i in range(bands)]
    beyond = [(i, i + 2) for i in range(1, bands - 2, 2)]
    beyond += [(i, i - 2) for i in range(2, bands, 2)]

    def sides(pair_block, cross_block):
        cross = lax.ppermute(cross_block, "band", across)
        pair = lax.ppermute(pair_block, "band", within)
        return pair, cross

    small = pltpu.SemaphoreType.DMA((5,)), pltpu.VMEM((16, 128), F32)
    inputs = (grid_state, mesh_state, enc_recv.T, proc_send.T, long_send)
    inputs = [pltpu.with_memory_space_constraint(x, pltpu.HBM) for x in inputs]
    buffers = [pltpu.VMEM(x.shape, jnp.int32) for x in inputs[2:]]
    (packed,) = kernel(
        pack_kernel,
        "pack",
        inputs,
        [((192, width), BF)],
        [*buffers, small[1], small[0]],
        products=8000,
        spaces=[HBM] * 5,
    )
    with jax.named_scope("mesh_sides"):
        pair_state, cross_state = sides(mesh_state, mesh_state)
        packed = packed.at[144:176].set(jnp.concatenate([pair_state, cross_state], axis=0))
    with jax.named_scope("gather_lon"):
        packed = lax.all_gather(packed, "lon", axis=0)
    sent, hot, spread = kernel(
        encode_first_kernel,
        "encode_first",
        (packed, edge_weights),
        [((512, width), F32), ((1024, 192), BF), ((192, 1024), BF)],
        products=1000,
    )
    acc, p1, far, p2 = kernel(
        encode_kernel,
        "encode",
        (packed, sent, hot, spread, edge_weights),
        [((192, width), F32), ((128, width), BF), ((64, width), BF), ((128, width), BF)],
        [pltpu.VMEM((1024, width), BF)],
        products=8000,
    )
    with jax.named_scope("sum_pair"):
        r1 = lax.ppermute(p1, "band", within)
        r_far = lax.ppermute(far, "band", beyond)
    with jax.named_scope("sum_cross"):
        chip = acc[0:64] + r1[64:128].astype(F32)
        r2 = lax.ppermute(p2.at[64:128].set(chip.astype(BF)), "band", across)
    inner_one, hot = kernel(
        process_first_kernel,
        "process_first",
        (packed, node_weights, r_far),
        [((192, width), F32), ((416, 256), BF)],
        products=1000,
        spaces=[VMEM, VMEM, ANY],
    )
    recv, inner_grid, hot_grid = kernel(
        decode_first_kernel,
        "decode_first",
        (grid_state, dec_send.T, edge_weights, node_weights, r_far),
        [((128, width), F32), ((128, width), F32), ((384, 192), BF)],
        [pltpu.VMEM((8, 128), F32)],
        products=1000,
        spaces=[VMEM] * 4 + [ANY],
    )
    band_two, mesh_two = kernel(
        process_kernel,
        "process",
        (acc, r1, r2, r_far, packed, inner_one, hot, edge_weights, node_weights, recv),
        [((64, width), BF), ((16, width), BF)],
        products=8000,
        spaces=[VMEM] * 9 + [ANY],
    )
    with jax.named_scope("two_sides"):
        pair_two, cross_two = sides(band_two, band_two)
    (grid_out,) = kernel(
        decode_kernel,
        "decode",
        (grid_state, band_two, pair_two, cross_two, recv, inner_grid, hot_grid, edge_weights, node_weights),
        [((128, width), BF)],
        products=8000,
    )
    return (grid_out, mesh_two)


def solution(mesh):
    rows = P(("band", "lon"), None)
    in_specs = (rows, rows, P(), P(), rows, rows, rows, rows)
    return jax.shard_map(
        per_device, mesh=mesh, in_specs=in_specs, out_specs=(rows, rows), check_vma=False
    )
```

```python
import jax
import jax.numpy as jnp
from jax import lax
from jax.experimental import pallas as pl
from jax.experimental.pallas import tpu as pltpu
from jax.sharding import PartitionSpec as P

BF = jnp.bfloat16
F32 = jnp.float32
NONE = 384


def mm(a, b):
    return jnp.dot(a, b, preferred_element_type=F32)


def silu_of_half(half):
    return half + half * jnp.tanh(half)


def layer_norm(values):
    average = jnp.mean(values, axis=-1, keepdims=True)
    centred = values - average
    spread = jnp.mean(centred * centred, axis=-1, keepdims=True)
    return centred * lax.rsqrt(spread + 1e-05)


def update(state, inner, aggregate, w1, w2):
    inner = inner + mm(aggregate.astype(BF), w1)
    outer = layer_norm(mm(silu_of_half(0.5 * inner).astype(BF), w2))
    return (state.astype(F32) + outer).astype(BF)


def slot_of(target_band, band):
    step = jnp.where(band % 2 == 0, target_band - band, band - target_band)
    return jnp.where(step < 0, 2, step)


def one_hot(index, rows, dtype=BF):
    lanes = lax.broadcasted_iota(jnp.int32, (index.shape[0], rows), 1)
    return jnp.where(lanes == index, 1.0, 0.0).astype(dtype)


def pack_kernel(grid_ref, mesh_ref, enc_ref, proc_ref, far_ref, out_ref, enc_buf, proc_buf, far_buf, rows, sems):
    small = [
        pltpu.make_async_copy(src, dst, sems.at[n])
        for n, (src, dst) in enumerate(((enc_ref, enc_buf), (proc_ref, proc_buf), (far_ref, far_buf)))
    ]
    large = []
    large.append(pltpu.make_async_copy(grid_ref, out_ref.at[0:128], sems.at[3]))
    large.append(pltpu.make_async_copy(mesh_ref, out_ref.at[128:144], sems.at[4]))
    for copy in small + large:
        copy.start()
    band = lax.axis_index("band")
    rows[...] = jnp.full(rows.shape, float(NONE), F32)
    for copy in small:
        copy.wait()
    enc = enc_buf[...]
    rows[0:2, :] = (slot_of(enc >> 6, band) * 64 + (enc & 63)).astype(F32)
    proc = proc_buf[...]
    rows[2:8, 0:16] = (slot_of(proc >> 6, band) * 64 + (proc & 63)).astype(F32)
    far = far_buf[...]
    rows[8:9, 0:6] = (slot_of(far >> 2, band) * 64 + (far & 3) * 16).astype(F32)
    index = rows[...].astype(BF)
    out_ref[176:192, 0:128] = index
    out_ref[176:192, 128:512] = jnp.zeros((16, 384), BF)
    for copy in large:
        copy.wait()


def window(all_ref):
    return jnp.concatenate(
        [all_ref[l, 128 + 16 * s : 144 + 16 * s] for s in range(3) for l in range(4)], axis=0
    )


def encode_first_kernel(all_ref, ew_ref, sent_ref, hot_ref, spread_ref):
    rows_id = lax.broadcasted_iota(jnp.int32, (192, 128), 0)
    for l in range(4):
        sent_ref[l * 128 : (l + 1) * 128] = 0.5 * mm(all_ref[l, 0:128], ew_ref[0, 0])
        index = all_ref[l, 176:192, 0:128].astype(F32)
        cols = index.T.astype(jnp.int32)
        flat = index.astype(jnp.int32)
        for k in range(2):
            start = l * 256 + k * 128
            spread_ref[:, start : start + 128] = jnp.where(rows_id == flat[k : k + 1, :], 1.0, 0.0).astype(BF)
            hot_ref[start : start + 128] = one_hot(cols[:, k : k + 1], 192)


def encode_kernel(all_ref, sent_ref, hot_ref, spread_ref, ew_ref, acc_ref, p1_ref, far_ref, p2_ref):
    table = window(all_ref)
    recv = (0.5 * mm(table, ew_ref[0, 1])).astype(BF)
    for l in range(4):
        sent = sent_ref[l * 128 : (l + 1) * 128]
        before = mm(hot_ref[l * 256 : (l + 1) * 256], recv) + jnp.concatenate([sent, sent], axis=0)
        result = layer_norm(mm(silu_of_half(before).astype(BF), ew_ref[0, 2]))
        part = mm(spread_ref[:, l * 256 : (l + 1) * 256], result.astype(BF))
        total = part if l == 0 else total + part
    acc_ref[...] = total
    p1_ref[...] = total[0:128].astype(BF)
    cross = total[128:192].astype(BF)
    far_ref[...] = cross
    p2_ref[0:64] = cross
    p2_ref[64:128] = cross


def process_first_kernel(all_ref, acc_ref, r1_ref, far_ref, ew_ref, nw_ref, inner_ref, send_ref, hots):
    near_id = lax.broadcasted_iota(jnp.int32, (16, 1), 0)
    lanes = lax.broadcasted_iota(jnp.int32, (16, 256), 1)
    far = []
    for l in range(4):
        cols = all_ref[l, 176:192, 0:128].astype(F32).T.astype(jnp.int32)
        for k in range(6):
            hit = jnp.logical_or(lanes == cols[0:16, 2 + k : 3 + k], lanes == near_id + (192 + 16 * l))
            hots[l * 96 + 16 * k : l * 96 + 16 * k + 16] = jnp.where(hit, 1.0, 0.0).astype(BF)
        far.append(jnp.logical_or(lanes[0:8] == cols[0:8, 8:9], lanes[0:8] == 192 + 16 * l))
    hots[384:416] = jnp.concatenate([jnp.where(hit, 1.0, 0.0) for hit in far], axis=0).astype(BF)
    table = window(all_ref)
    inner = mm(table, nw_ref[0, 0])
    inner_ref[...] = jnp.concatenate([inner[0:64], inner[128:192]], axis=0)
    sums = acc_ref[64:128] + r1_ref[0:64].astype(F32) + far_ref[...].astype(F32)
    one = update(table[64:128], inner[64:128], sums, nw_ref[0, 1], nw_ref[0, 2])
    send_ref[...] = (0.5 * mm(one, ew_ref[1, 0])).astype(BF)


def process_kernel(
    acc_ref, r1_ref, r2_ref, send_ref, all_ref, inner_ref, hots, ew_ref, nw_ref, after_ref, band_ref, own_ref
):
    table = window(all_ref)
    table = jnp.concatenate([table[0:64], table[128:192]], axis=0)
    own = acc_ref[0:64] + r1_ref[64:128].astype(F32) + r2_ref[0:64].astype(F32)
    cross = acc_ref[128:192] + r2_ref[64:128].astype(F32)
    sums = jnp.concatenate([own, cross], axis=0)
    one = update(table, inner_ref[...], sums, nw_ref[0, 1], nw_ref[0, 2])
    send = (0.5 * mm(one, ew_ref[1, 0])).astype(BF)
    recv = (0.5 * mm(one[0:64], ew_ref[1, 1])).astype(BF)
    both = jnp.concatenate([send[0:64], send_ref[...], send[64:128], recv], axis=0)
    inner = mm(one[0:64], nw_ref[1, 0])
    near_id = lax.broadcasted_iota(jnp.int32, (16, 1), 0)
    far_id = lax.broadcasted_iota(jnp.int32, (8, 1), 0)
    near, far = [], []
    for start, size in ((0, 192), (192, 224)):
        before = mm(hots[start : start + size], both)
        messages = layer_norm(mm(silu_of_half(before).astype(BF), ew_ref[1, 2]))
        for m in range(2):
            total = messages[96 * m : 96 * m + 16]
            for k in range(1, 6):
                total = total + messages[96 * m + 16 * k : 96 * m + 16 * k + 16]
            near.append(total)
    for l in range(4):
        values = jnp.where(far_id < 6, messages[192 + 8 * l : 200 + 8 * l], 0.0)
        far.append(jnp.sum(values, axis=0, keepdims=True))
    parts = [a + jnp.where(near_id == 0, b, 0.0) for a, b in zip(near, far)]
    sums = jnp.concatenate(parts, axis=0)
    two = update(one[0:64], inner, sums, nw_ref[1, 1], nw_ref[1, 2])
    band_ref[...] = two
    lon = lax.axis_index("lon")
    for l in range(4):

        @pl.when(lon == l)
        def _():
            own_ref[...] = two[16 * l : 16 * l + 16]


def decode_first_kernel(grid_ref, dec_ref, ew_ref, nw_ref, after_ref, recv_ref, inner_ref, hots, rows):
    index = dec_ref[...]
    rows[...] = jnp.zeros(rows.shape, F32)
    rows[0:3, :] = (slot_of(index >> 6, lax.axis_index("band")) * 64 + (index & 63)).astype(F32)
    index = rows[...].T.astype(jnp.int32)
    for k in range(3):
        hots[k * 128 : (k + 1) * 128] = one_hot(index[:, k : k + 1], 192)
    recv_ref[...] = 0.5 * mm(grid_ref[...], ew_ref[2, 1])
    inner_ref[...] = mm(grid_ref[...], nw_ref[2, 0])


def decode_kernel(grid_ref, own_ref, pair_ref, cross_ref, recv_ref, inner_ref, hots, ew_ref, nw_ref, out_ref):
    table = jnp.concatenate([own_ref[...], pair_ref[...], cross_ref[...]], axis=0)
    send = (0.5 * mm(table, ew_ref[2, 0])).astype(BF)
    recv = recv_ref[...]
    sums = None
    for k in range(3):
        before = mm(hots[k * 128 : (k + 1) * 128], send) + recv
        messages = layer_norm(mm(silu_of_half(before).astype(BF), ew_ref[2, 2]))
        sums = messages if sums is None else sums + messages
    out_ref[...] = update(grid_ref[...], inner_ref[...], sums, nw_ref[2, 1], nw_ref[2, 2])


VMEM = pl.BlockSpec(memory_space=pltpu.VMEM)
HBM = pl.BlockSpec(memory_space=pltpu.HBM)
ANY = pl.BlockSpec(memory_space=pl.ANY)
MIB = 1024 * 1024


def kernel(body, name, operands, outs, scratch=(), limit=16, products=4000, spaces=None):
    return pl.pallas_call(
        body,
        in_specs=spaces or [VMEM] * len(operands),
        out_specs=[VMEM] * len(outs),
        out_shape=[jax.ShapeDtypeStruct(dims, kind) for dims, kind in outs],
        scratch_shapes=list(scratch),
        compiler_params=pltpu.CompilerParams(vmem_limit_bytes=limit * MIB),
        cost_estimate=pl.CostEstimate(
            flops=2 * products * 512 * 512, bytes_accessed=8 * MIB, transcendentals=0
        ),
        name=name,
    )(*operands)


def per_device(
    grid_state, mesh_state, edge_weights, node_weights, enc_recv, proc_send, long_send, dec_send
):
    width = grid_state.shape[1]
    bands = lax.axis_size("band")
    across = [(i, i + 1 if i % 2 else i - 1) for i in range(1, bands - 1)]
    within = [(i, i ^ 1) for i in range(bands)]
    beyond = [(i, i + 2) for i in range(1, bands - 2, 2)]
    beyond += [(i, i - 2) for i in range(2, bands, 2)]

    def sides(pair_block, cross_block):
        cross = lax.ppermute(cross_block, "band", across)
        pair = lax.ppermute(pair_block, "band", within)
        return pair, cross

    small = pltpu.SemaphoreType.DMA((5,)), pltpu.VMEM((16, 128), F32)
    inputs = (grid_state, mesh_state, enc_recv.T, proc_send.T, long_send)
    inputs = [pltpu.with_memory_space_constraint(x, pltpu.HBM) for x in inputs]
    buffers = [pltpu.VMEM(x.shape, jnp.int32) for x in inputs[2:]]
    (packed,) = kernel(
        pack_kernel,
        "pack",
        inputs,
        [((192, width), BF)],
        [*buffers, small[1], small[0]],
        products=8000,
        spaces=[HBM] * 5,
    )
    with jax.named_scope("mesh_sides"):
        pair_state, cross_state = sides(mesh_state, mesh_state)
        packed = packed.at[144:176].set(jnp.concatenate([pair_state, cross_state], axis=0))
    with jax.named_scope("gather_lon"):
        packed = lax.all_gather(packed, "lon", axis=0)
    sent, hot, spread = kernel(
        encode_first_kernel,
        "encode_first",
        (packed, edge_weights),
        [((512, width), F32), ((1024, 192), BF), ((192, 1024), BF)],
        products=1000,
    )
    acc, p1, far, p2 = kernel(
        encode_kernel,
        "encode",
        (packed, sent, hot, spread, edge_weights),
        [((192, width), F32), ((128, width), BF), ((64, width), BF), ((128, width), BF)],
        products=8000,
    )
    with jax.named_scope("sum_pair"):
        r1 = lax.ppermute(p1, "band", within)
        r_far = lax.ppermute(far, "band", beyond)
    with jax.named_scope("sum_cross"):
        chip = acc[0:64] + r1[64:128].astype(F32)
        r2 = lax.ppermute(p2.at[64:128].set(chip.astype(BF)), "band", across)
    inner_one, send_pair, hot = kernel(
        process_first_kernel,
        "process_first",
        (packed, acc, r1, r_far, edge_weights, node_weights),
        [((128, width), F32), ((64, width), BF), ((416, 256), BF)],
        products=1000,
    )
    recv, inner_grid, hot_grid = kernel(
        decode_first_kernel,
        "decode_first",
        (grid_state, dec_send.T, edge_weights, node_weights, r_far),
        [((128, width), F32), ((128, width), F32), ((384, 192), BF)],
        [pltpu.VMEM((8, 128), F32)],
        products=1000,
        spaces=[VMEM] * 4 + [ANY],
    )
    band_two, mesh_two = kernel(
        process_kernel,
        "process",
        (acc, r1, r2, send_pair, packed, inner_one, hot, edge_weights, node_weights, recv),
        [((64, width), BF), ((16, width), BF)],
        products=8000,
        spaces=[VMEM] * 9 + [ANY],
    )
    with jax.named_scope("two_sides"):
        pair_two, cross_two = sides(band_two, band_two)
    (grid_out,) = kernel(
        decode_kernel,
        "decode",
        (grid_state, band_two, pair_two, cross_two, recv, inner_grid, hot_grid, edge_weights, node_weights),
        [((128, width), BF)],
        products=8000,
    )
    return (grid_out, mesh_two)


def solution(mesh):
    rows = P(("band", "lon"), None)
    in_specs = (rows, rows, P(), P(), rows, rows, rows, rows)
    return jax.shard_map(
        per_device, mesh=mesh, in_specs=in_specs, out_specs=(rows, rows), check_vma=False
    )
```

```python
import jax
import jax.numpy as jnp
from jax import lax
from jax.experimental import pallas as pl
from jax.experimental.pallas import tpu as pltpu
from jax.sharding import PartitionSpec as P

BF = jnp.bfloat16
F32 = jnp.float32
NONE = 384


def mm(a, b):
    return jnp.dot(a, b, preferred_element_type=F32)


def silu_of_half(half):
    return half + half * jnp.tanh(half)


def layer_norm(values):
    average = jnp.mean(values, axis=-1, keepdims=True)
    centred = values - average
    spread = jnp.mean(centred * centred, axis=-1, keepdims=True)
    return centred * lax.rsqrt(spread + 1e-05)


def update(state, inner, aggregate, w1, w2):
    inner = inner + mm(aggregate.astype(BF), w1)
    outer = layer_norm(mm(silu_of_half(0.5 * inner).astype(BF), w2))
    return (state.astype(F32) + outer).astype(BF)


def slot_of(target_band, band):
    step = jnp.where(band % 2 == 0, target_band - band, band - target_band)
    return jnp.where(step < 0, 2, step)


def one_hot(index, rows, dtype=BF):
    lanes = lax.broadcasted_iota(jnp.int32, (index.shape[0], rows), 1)
    return jnp.where(lanes == index, 1.0, 0.0).astype(dtype)


def pack_kernel(grid_ref, mesh_ref, enc_ref, proc_ref, far_ref, out_ref, enc_buf, proc_buf, far_buf, rows, sems):
    small = [
        pltpu.make_async_copy(src, dst, sems.at[n])
        for n, (src, dst) in enumerate(((enc_ref, enc_buf), (proc_ref, proc_buf), (far_ref, far_buf)))
    ]
    large = []
    large.append(pltpu.make_async_copy(grid_ref, out_ref.at[0:128], sems.at[3]))
    large.append(pltpu.make_async_copy(mesh_ref, out_ref.at[128:144], sems.at[4]))
    for copy in small + large:
        copy.start()
    band = lax.axis_index("band")
    rows[...] = jnp.full(rows.shape, float(NONE), F32)
    for copy in small:
        copy.wait()
    enc = enc_buf[...]
    rows[0:2, :] = (slot_of(enc >> 6, band) * 64 + (enc & 63)).astype(F32)
    proc = proc_buf[...]
    rows[2:8, 0:16] = (slot_of(proc >> 6, band) * 64 + (proc & 63)).astype(F32)
    far = far_buf[...]
    rows[8:9, 0:6] = (slot_of(far >> 2, band) * 64 + (far & 3) * 16).astype(F32)
    index = rows[...].astype(BF)
    out_ref[176:192, 0:128] = index
    out_ref[176:192, 128:512] = jnp.zeros((16, 384), BF)
    for copy in large:
        copy.wait()


def window(all_ref):
    return jnp.concatenate(
        [all_ref[l, 128 + 16 * s : 144 + 16 * s] for s in range(3) for l in range(4)], axis=0
    )


def encode_first_kernel(all_ref, ew_ref, sent_ref, hot_ref, spread_ref):
    rows_id = lax.broadcasted_iota(jnp.int32, (192, 128), 0)
    grid_rows = jnp.concatenate([all_ref[l, 0:128] for l in range(4)], axis=0)
    sent_ref[...] = 0.5 * mm(grid_rows, ew_ref[0, 0])
    for l in range(4):
        index = all_ref[l, 176:192, 0:128].astype(F32)
        cols = index.T.astype(jnp.int32)
        flat = index.astype(jnp.int32)
        for k in range(2):
            start = l * 256 + k * 128
            spread_ref[:, start : start + 128] = jnp.where(rows_id == flat[k : k + 1, :], 1.0, 0.0).astype(BF)
            hot_ref[start : start + 128] = one_hot(cols[:, k : k + 1], 192)


def encode_kernel(all_ref, sent_ref, hot_ref, spread_ref, ew_ref, acc_ref, p1_ref, far_ref, p2_ref, msgs):
    table = window(all_ref)
    recv = (0.5 * mm(table, ew_ref[0, 1])).astype(BF)
    for n in range(2):
        sent = [sent_ref[l * 128 : (l + 1) * 128] for l in (2 * n, 2 * n, 2 * n + 1, 2 * n + 1)]
        before = mm(hot_ref[n * 512 : (n + 1) * 512], recv) + jnp.concatenate(sent, axis=0)
        result = layer_norm(mm(silu_of_half(before).astype(BF), ew_ref[0, 2]))
        msgs[n * 512 : (n + 1) * 512] = result.astype(BF)
    total = mm(spread_ref[...], msgs[...])
    acc_ref[...] = total
    p1_ref[...] = total[0:128].astype(BF)
    cross = total[128:192].astype(BF)
    far_ref[...] = cross
    p2_ref[0:64] = cross
    p2_ref[64:128] = cross


def process_first_kernel(all_ref, acc_ref, r1_ref, far_ref, ew_ref, nw_ref, inner_ref, send_ref, hots):
    near_id = lax.broadcasted_iota(jnp.int32, (16, 1), 0)
    lanes = lax.broadcasted_iota(jnp.int32, (16, 256), 1)
    far = []
    for l in range(4):
        cols = all_ref[l, 176:192, 0:128].astype(F32).T.astype(jnp.int32)
        for k in range(6):
            hit = jnp.logical_or(lanes == cols[0:16, 2 + k : 3 + k], lanes == near_id + (192 + 16 * l))
            hots[l * 96 + 16 * k : l * 96 + 16 * k + 16] = jnp.where(hit, 1.0, 0.0).astype(BF)
        far.append(jnp.logical_or(lanes[0:8] == cols[0:8, 8:9], lanes[0:8] == 192 + 16 * l))
    hots[384:416] = jnp.concatenate([jnp.where(hit, 1.0, 0.0) for hit in far], axis=0).astype(BF)
    table = window(all_ref)
    inner = mm(table, nw_ref[0, 0])
    inner_ref[...] = jnp.concatenate([inner[0:64], inner[128:192]], axis=0)
    sums = acc_ref[64:128] + r1_ref[0:64].astype(F32) + far_ref[...].astype(F32)
    one = update(table[64:128], inner[64:128], sums, nw_ref[0, 1], nw_ref[0, 2])
    send_ref[...] = (0.5 * mm(one, ew_ref[1, 0])).astype(BF)


def process_kernel(
    acc_ref, r1_ref, r2_ref, send_ref, all_ref, inner_ref, hots, ew_ref, nw_ref, after_ref, band_ref, own_ref
):
    table = window(all_ref)
    table = jnp.concatenate([table[0:64], table[128:192]], axis=0)
    own = acc_ref[0:64] + r1_ref[64:128].astype(F32) + r2_ref[0:64].astype(F32)
    cross = acc_ref[128:192] + r2_ref[64:128].astype(F32)
    sums = jnp.concatenate([own, cross], axis=0)
    one = update(table, inner_ref[...], sums, nw_ref[0, 1], nw_ref[0, 2])
    send = (0.5 * mm(one, ew_ref[1, 0])).astype(BF)
    recv = (0.5 * mm(one[0:64], ew_ref[1, 1])).astype(BF)
    both = jnp.concatenate([send[0:64], send_ref[...], send[64:128], recv], axis=0)
    inner = mm(one[0:64], nw_ref[1, 0])
    near_id = lax.broadcasted_iota(jnp.int32, (16, 1), 0)
    far_id = lax.broadcasted_iota(jnp.int32, (8, 1), 0)
    near, far = [], []
    before = mm(hots[...], both)
    messages = layer_norm(mm(silu_of_half(before).astype(BF), ew_ref[1, 2]))
    for l in range(4):
        total = messages[96 * l : 96 * l + 16]
        for k in range(1, 6):
            total = total + messages[96 * l + 16 * k : 96 * l + 16 * k + 16]
        near.append(total)
    for l in range(4):
        values = jnp.where(far_id < 6, messages[384 + 8 * l : 392 + 8 * l], 0.0)
        far.append(jnp.sum(values, axis=0, keepdims=True))
    parts = [a + jnp.where(near_id == 0, b, 0.0) for a, b in zip(near, far)]
    sums = jnp.concatenate(parts, axis=0)
    two = update(one[0:64], inner, sums, nw_ref[1, 1], nw_ref[1, 2])
    band_ref[...] = two
    lon = lax.axis_index("lon")
    for l in range(4):

        @pl.when(lon == l)
        def _():
            own_ref[...] = two[16 * l : 16 * l + 16]


def decode_first_kernel(grid_ref, dec_ref, ew_ref, nw_ref, after_ref, recv_ref, inner_ref, hots, rows):
    index = dec_ref[...]
    rows[...] = jnp.zeros(rows.shape, F32)
    rows[0:3, :] = (slot_of(index >> 6, lax.axis_index("band")) * 64 + (index & 63)).astype(F32)
    index = rows[...].T.astype(jnp.int32)
    for k in range(3):
        hots[k * 128 : (k + 1) * 128] = one_hot(index[:, k : k + 1], 192)
    recv_ref[...] = 0.5 * mm(grid_ref[...], ew_ref[2, 1])
    inner_ref[...] = mm(grid_ref[...], nw_ref[2, 0])


def decode_kernel(grid_ref, own_ref, pair_ref, cross_ref, recv_ref, inner_ref, hots, ew_ref, nw_ref, out_ref):
    table = jnp.concatenate([own_ref[...], pair_ref[...], cross_ref[...]], axis=0)
    send = (0.5 * mm(table, ew_ref[2, 0])).astype(BF)
    recv = recv_ref[...]
    before = mm(hots[...], send) + jnp.concatenate([recv, recv, recv], axis=0)
    messages = layer_norm(mm(silu_of_half(before).astype(BF), ew_ref[2, 2]))
    sums = messages[0:128] + messages[128:256] + messages[256:384]
    out_ref[...] = update(grid_ref[...], inner_ref[...], sums, nw_ref[2, 1], nw_ref[2, 2])


VMEM = pl.BlockSpec(memory_space=pltpu.VMEM)
HBM = pl.BlockSpec(memory_space=pltpu.HBM)
ANY = pl.BlockSpec(memory_space=pl.ANY)
MIB = 1024 * 1024


def kernel(body, name, operands, outs, scratch=(), limit=16, products=4000, spaces=None):
    return pl.pallas_call(
        body,
        in_specs=spaces or [VMEM] * len(operands),
        out_specs=[VMEM] * len(outs),
        out_shape=[jax.ShapeDtypeStruct(dims, kind) for dims, kind in outs],
        scratch_shapes=list(scratch),
        compiler_params=pltpu.CompilerParams(vmem_limit_bytes=limit * MIB),
        cost_estimate=pl.CostEstimate(
            flops=2 * products * 512 * 512, bytes_accessed=8 * MIB, transcendentals=0
        ),
        name=name,
    )(*operands)


def per_device(
    grid_state, mesh_state, edge_weights, node_weights, enc_recv, proc_send, long_send, dec_send
):
    width = grid_state.shape[1]
    bands = lax.axis_size("band")
    across = [(i, i + 1 if i % 2 else i - 1) for i in range(1, bands - 1)]
    within = [(i, i ^ 1) for i in range(bands)]
    beyond = [(i, i + 2) for i in range(1, bands - 2, 2)]
    beyond += [(i, i - 2) for i in range(2, bands, 2)]

    def sides(pair_block, cross_block):
        cross = lax.ppermute(cross_block, "band", across)
        pair = lax.ppermute(pair_block, "band", within)
        return pair, cross

    small = pltpu.SemaphoreType.DMA((5,)), pltpu.VMEM((16, 128), F32)
    inputs = (grid_state, mesh_state, enc_recv.T, proc_send.T, long_send)
    inputs = [pltpu.with_memory_space_constraint(x, pltpu.HBM) for x in inputs]
    buffers = [pltpu.VMEM(x.shape, jnp.int32) for x in inputs[2:]]
    (packed,) = kernel(
        pack_kernel,
        "pack",
        inputs,
        [((192, width), BF)],
        [*buffers, small[1], small[0]],
        products=8000,
        spaces=[HBM] * 5,
    )
    with jax.named_scope("mesh_sides"):
        pair_state, cross_state = sides(mesh_state, mesh_state)
        packed = packed.at[144:176].set(jnp.concatenate([pair_state, cross_state], axis=0))
    with jax.named_scope("gather_lon"):
        packed = lax.all_gather(packed, "lon", axis=0)
    sent, hot, spread = kernel(
        encode_first_kernel,
        "encode_first",
        (packed, edge_weights),
        [((512, width), F32), ((1024, 192), BF), ((192, 1024), BF)],
        products=1000,
    )
    acc, p1, far, p2 = kernel(
        encode_kernel,
        "encode",
        (packed, sent, hot, spread, edge_weights),
        [((192, width), F32), ((128, width), BF), ((64, width), BF), ((128, width), BF)],
        [pltpu.VMEM((1024, width), BF)],
        products=8000,
    )
    with jax.named_scope("sum_pair"):
        r1 = lax.ppermute(p1, "band", within)
        r_far = lax.ppermute(far, "band", beyond)
    with jax.named_scope("sum_cross"):
        chip = acc[0:64] + r1[64:128].astype(F32)
        r2 = lax.ppermute(p2.at[64:128].set(chip.astype(BF)), "band", across)
    inner_one, send_pair, hot = kernel(
        process_first_kernel,
        "process_first",
        (packed, acc, r1, r_far, edge_weights, node_weights),
        [((128, width), F32), ((64, width), BF), ((416, 256), BF)],
        products=1000,
    )
    recv, inner_grid, hot_grid = kernel(
        decode_first_kernel,
        "decode_first",
        (grid_state, dec_send.T, edge_weights, node_weights, r_far),
        [((128, width), F32), ((128, width), F32), ((384, 192), BF)],
        [pltpu.VMEM((8, 128), F32)],
        products=1000,
        spaces=[VMEM] * 4 + [ANY],
    )
    band_two, mesh_two = kernel(
        process_kernel,
        "process",
        (acc, r1, r2, send_pair, packed, inner_one, hot, edge_weights, node_weights, recv),
        [((64, width), BF), ((16, width), BF)],
        products=8000,
        spaces=[VMEM] * 9 + [ANY],
    )
    with jax.named_scope("two_sides"):
        pair_two, cross_two = sides(band_two, band_two)
    (grid_out,) = kernel(
        decode_kernel,
        "decode",
        (grid_state, band_two, pair_two, cross_two, recv, inner_grid, hot_grid, edge_weights, node_weights),
        [((128, width), BF)],
        products=8000,
    )
    return (grid_out, mesh_two)


def solution(mesh):
    rows = P(("band", "lon"), None)
    in_specs = (rows, rows, P(), P(), rows, rows, rows, rows)
    return jax.shard_map(
        per_device, mesh=mesh, in_specs=in_specs, out_specs=(rows, rows), check_vma=False
    )
```

```python
import jax
import jax.numpy as jnp
from jax import lax
from jax.experimental import pallas as pl
from jax.experimental.pallas import tpu as pltpu
from jax.sharding import PartitionSpec as P

BF = jnp.bfloat16
F32 = jnp.float32
NONE = 384


def mm(a, b):
    return jnp.dot(a, b, preferred_element_type=F32)


def silu_of_half(half):
    return half + half * jnp.tanh(half)


def layer_norm(values):
    average = jnp.mean(values, axis=-1, keepdims=True)
    centred = values - average
    spread = jnp.mean(centred * centred, axis=-1, keepdims=True)
    return centred * lax.rsqrt(spread + 1e-05)


def update(state, inner, aggregate, w1, w2):
    inner = inner + mm(aggregate.astype(BF), w1)
    outer = layer_norm(mm(silu_of_half(0.5 * inner).astype(BF), w2))
    return (state.astype(F32) + outer).astype(BF)


def slot_of(target_band, band):
    step = jnp.where(band % 2 == 0, target_band - band, band - target_band)
    return jnp.where(step < 0, 2, step)


def one_hot(index, rows, dtype=BF):
    lanes = lax.broadcasted_iota(jnp.int32, (index.shape[0], rows), 1)
    return jnp.where(lanes == index, 1.0, 0.0).astype(dtype)


def pack_kernel(grid_ref, mesh_ref, enc_ref, proc_ref, far_ref, out_ref, enc_buf, proc_buf, far_buf, rows, sems):
    small = [
        pltpu.make_async_copy(src, dst, sems.at[n])
        for n, (src, dst) in enumerate(((enc_ref, enc_buf), (proc_ref, proc_buf), (far_ref, far_buf)))
    ]
    large = []
    large.append(pltpu.make_async_copy(grid_ref, out_ref.at[0:128], sems.at[3]))
    large.append(pltpu.make_async_copy(mesh_ref, out_ref.at[128:144], sems.at[4]))
    for copy in small + large:
        copy.start()
    band = lax.axis_index("band")
    rows[...] = jnp.full(rows.shape, float(NONE), F32)
    for copy in small:
        copy.wait()
    enc = enc_buf[...]
    rows[0:2, :] = (slot_of(enc >> 6, band) * 64 + (enc & 63)).astype(F32)
    proc = proc_buf[...]
    rows[2:8, 0:16] = (slot_of(proc >> 6, band) * 64 + (proc & 63)).astype(F32)
    far = far_buf[...]
    rows[8:9, 0:6] = (slot_of(far >> 2, band) * 64 + (far & 3) * 16).astype(F32)
    index = rows[...].astype(BF)
    out_ref[160:176, 0:128] = index
    out_ref[160:176, 128:512] = jnp.zeros((16, 384), BF)
    for copy in large:
        copy.wait()


def mesh_rows(all_ref, start):
    return jnp.concatenate([all_ref[l, start : start + 16] for l in range(4)], axis=0)


def window(all_ref, pair_ref):
    return jnp.concatenate([mesh_rows(all_ref, 128), pair_ref[...], mesh_rows(all_ref, 144)], axis=0)


def encode_first_kernel(all_ref, ew_ref, sent_ref, hot_ref, spread_ref):
    rows_id = lax.broadcasted_iota(jnp.int32, (192, 128), 0)
    grid_rows = jnp.concatenate([all_ref[l, 0:128] for l in range(4)], axis=0)
    sent_ref[...] = 0.5 * mm(grid_rows, ew_ref[0, 0])
    for l in range(4):
        index = all_ref[l, 160:176, 0:128].astype(F32)
        cols = index.T.astype(jnp.int32)
        flat = index.astype(jnp.int32)
        for k in range(2):
            start = l * 256 + k * 128
            spread_ref[:, start : start + 128] = jnp.where(rows_id == flat[k : k + 1, :], 1.0, 0.0).astype(BF)
            hot_ref[start : start + 128] = one_hot(cols[:, k : k + 1], 192)


def encode_kernel(all_ref, pair_ref, sent_ref, hot_ref, spread_ref, ew_ref, acc_ref, p1_ref, far_ref, p2_ref, msgs):
    table = window(all_ref, pair_ref)
    recv = (0.5 * mm(table, ew_ref[0, 1])).astype(BF)
    for n in range(2):
        sent = [sent_ref[l * 128 : (l + 1) * 128] for l in (2 * n, 2 * n, 2 * n + 1, 2 * n + 1)]
        before = mm(hot_ref[n * 512 : (n + 1) * 512], recv) + jnp.concatenate(sent, axis=0)
        result = layer_norm(mm(silu_of_half(before).astype(BF), ew_ref[0, 2]))
        msgs[n * 512 : (n + 1) * 512] = result.astype(BF)
    total = mm(spread_ref[...], msgs[...])
    acc_ref[...] = total
    p1_ref[...] = total[0:128].astype(BF)
    cross = total[128:192].astype(BF)
    far_ref[...] = cross
    p2_ref[0:64] = cross
    p2_ref[64:128] = cross


def process_first_kernel(all_ref, pair_ref, acc_ref, r1_ref, far_ref, ew_ref, nw_ref, inner_ref, send_ref, hots):
    near_id = lax.broadcasted_iota(jnp.int32, (16, 1), 0)
    lanes = lax.broadcasted_iota(jnp.int32, (16, 256), 1)
    far = []
    for l in range(4):
        cols = all_ref[l, 160:176, 0:128].astype(F32).T.astype(jnp.int32)
        for k in range(6):
            hit = jnp.logical_or(lanes == cols[0:16, 2 + k : 3 + k], lanes == near_id + (192 + 16 * l))
            hots[l * 96 + 16 * k : l * 96 + 16 * k + 16] = jnp.where(hit, 1.0, 0.0).astype(BF)
        far.append(jnp.logical_or(lanes[0:8] == cols[0:8, 8:9], lanes[0:8] == 192 + 16 * l))
    hots[384:416] = jnp.concatenate([jnp.where(hit, 1.0, 0.0) for hit in far], axis=0).astype(BF)
    table = window(all_ref, pair_ref)
    inner = mm(table, nw_ref[0, 0])
    inner_ref[...] = jnp.concatenate([inner[0:64], inner[128:192]], axis=0)
    sums = acc_ref[64:128] + r1_ref[0:64].astype(F32) + far_ref[...].astype(F32)
    one = update(table[64:128], inner[64:128], sums, nw_ref[0, 1], nw_ref[0, 2])
    send_ref[...] = (0.5 * mm(one, ew_ref[1, 0])).astype(BF)


def process_kernel(
    acc_ref, r1_ref, r2_ref, send_ref, all_ref, inner_ref, hots, ew_ref, nw_ref, after_ref, band_ref, own_ref
):
    table = jnp.concatenate([mesh_rows(all_ref, 128), mesh_rows(all_ref, 144)], axis=0)
    own = acc_ref[0:64] + r1_ref[64:128].astype(F32) + r2_ref[0:64].astype(F32)
    cross = acc_ref[128:192] + r2_ref[64:128].astype(F32)
    sums = jnp.concatenate([own, cross], axis=0)
    one = update(table, inner_ref[...], sums, nw_ref[0, 1], nw_ref[0, 2])
    send = (0.5 * mm(one, ew_ref[1, 0])).astype(BF)
    recv = (0.5 * mm(one[0:64], ew_ref[1, 1])).astype(BF)
    both = jnp.concatenate([send[0:64], send_ref[...], send[64:128], recv], axis=0)
    inner = mm(one[0:64], nw_ref[1, 0])
    near_id = lax.broadcasted_iota(jnp.int32, (16, 1), 0)
    far_id = lax.broadcasted_iota(jnp.int32, (8, 1), 0)
    near, far = [], []
    before = mm(hots[...], both)
    messages = layer_norm(mm(silu_of_half(before).astype(BF), ew_ref[1, 2]))
    for l in range(4):
        total = messages[96 * l : 96 * l + 16]
        for k in range(1, 6):
            total = total + messages[96 * l + 16 * k : 96 * l + 16 * k + 16]
        near.append(total)
    for l in range(4):
        values = jnp.where(far_id < 6, messages[384 + 8 * l : 392 + 8 * l], 0.0)
        far.append(jnp.sum(values, axis=0, keepdims=True))
    parts = [a + jnp.where(near_id == 0, b, 0.0) for a, b in zip(near, far)]
    sums = jnp.concatenate(parts, axis=0)
    two = update(one[0:64], inner, sums, nw_ref[1, 1], nw_ref[1, 2])
    band_ref[...] = two
    lon = lax.axis_index("lon")
    for l in range(4):

        @pl.when(lon == l)
        def _():
            own_ref[...] = two[16 * l : 16 * l + 16]


def decode_first_kernel(grid_ref, dec_ref, ew_ref, nw_ref, after_ref, recv_ref, inner_ref, hots, rows):
    index = dec_ref[...]
    rows[...] = jnp.zeros(rows.shape, F32)
    rows[0:3, :] = (slot_of(index >> 6, lax.axis_index("band")) * 64 + (index & 63)).astype(F32)
    index = rows[...].T.astype(jnp.int32)
    for k in range(3):
        hots[k * 128 : (k + 1) * 128] = one_hot(index[:, k : k + 1], 192)
    recv_ref[...] = 0.5 * mm(grid_ref[...], ew_ref[2, 1])
    inner_ref[...] = mm(grid_ref[...], nw_ref[2, 0])


def decode_kernel(grid_ref, own_ref, pair_ref, cross_ref, recv_ref, inner_ref, hots, ew_ref, nw_ref, out_ref):
    table = jnp.concatenate([own_ref[...], pair_ref[...], cross_ref[...]], axis=0)
    send = (0.5 * mm(table, ew_ref[2, 0])).astype(BF)
    recv = recv_ref[...]
    before = mm(hots[...], send) + jnp.concatenate([recv, recv, recv], axis=0)
    messages = layer_norm(mm(silu_of_half(before).astype(BF), ew_ref[2, 2]))
    sums = messages[0:128] + messages[128:256] + messages[256:384]
    out_ref[...] = update(grid_ref[...], inner_ref[...], sums, nw_ref[2, 1], nw_ref[2, 2])


VMEM = pl.BlockSpec(memory_space=pltpu.VMEM)
HBM = pl.BlockSpec(memory_space=pltpu.HBM)
ANY = pl.BlockSpec(memory_space=pl.ANY)
MIB = 1024 * 1024


def kernel(body, name, operands, outs, scratch=(), limit=16, products=4000, spaces=None):
    return pl.pallas_call(
        body,
        in_specs=spaces or [VMEM] * len(operands),
        out_specs=[VMEM] * len(outs),
        out_shape=[jax.ShapeDtypeStruct(dims, kind) for dims, kind in outs],
        scratch_shapes=list(scratch),
        compiler_params=pltpu.CompilerParams(vmem_limit_bytes=limit * MIB),
        cost_estimate=pl.CostEstimate(
            flops=2 * products * 512 * 512, bytes_accessed=8 * MIB, transcendentals=0
        ),
        name=name,
    )(*operands)


def per_device(
    grid_state, mesh_state, edge_weights, node_weights, enc_recv, proc_send, long_send, dec_send
):
    width = grid_state.shape[1]
    bands = lax.axis_size("band")
    across = [(i, i + 1 if i % 2 else i - 1) for i in range(1, bands - 1)]
    within = [(i, i ^ 1) for i in range(bands)]
    beyond = [(i, i + 2) for i in range(1, bands - 2, 2)]
    beyond += [(i, i - 2) for i in range(2, bands, 2)]

    def sides(pair_block, cross_block):
        cross = lax.ppermute(cross_block, "band", across)
        pair = lax.ppermute(pair_block, "band", within)
        return pair, cross

    small = pltpu.SemaphoreType.DMA((5,)), pltpu.VMEM((16, 128), F32)
    inputs = (grid_state, mesh_state, enc_recv.T, proc_send.T, long_send)
    inputs = [pltpu.with_memory_space_constraint(x, pltpu.HBM) for x in inputs]
    buffers = [pltpu.VMEM(x.shape, jnp.int32) for x in inputs[2:]]
    (packed,) = kernel(
        pack_kernel,
        "pack",
        inputs,
        [((176, width), BF)],
        [*buffers, small[1], small[0]],
        products=8000,
        spaces=[HBM] * 5,
    )
    with jax.named_scope("mesh_cross"):
        packed = packed.at[144:160].set(lax.ppermute(mesh_state, "band", across))
    with jax.named_scope("gather_lon"):
        packed = lax.all_gather(packed, "lon", axis=0)
    with jax.named_scope("mesh_pair"):
        pair_state = lax.ppermute(packed[:, 128:144].reshape(64, width), "band", within)
    sent, hot, spread = kernel(
        encode_first_kernel,
        "encode_first",
        (packed, edge_weights),
        [((512, width), F32), ((1024, 192), BF), ((192, 1024), BF)],
        products=1000,
    )
    acc, p1, far, p2 = kernel(
        encode_kernel,
        "encode",
        (packed, pair_state, sent, hot, spread, edge_weights),
        [((192, width), F32), ((128, width), BF), ((64, width), BF), ((128, width), BF)],
        [pltpu.VMEM((1024, width), BF)],
        products=8000,
    )
    with jax.named_scope("sum_pair"):
        r1 = lax.ppermute(p1, "band", within)
        r_far = lax.ppermute(far, "band", beyond)
    with jax.named_scope("sum_cross"):
        chip = acc[0:64] + r1[64:128].astype(F32)
        r2 = lax.ppermute(p2.at[64:128].set(chip.astype(BF)), "band", across)
    inner_one, send_pair, hot = kernel(
        process_first_kernel,
        "process_first",
        (packed, pair_state, acc, r1, r_far, edge_weights, node_weights),
        [((128, width), F32), ((64, width), BF), ((416, 256), BF)],
        products=1000,
    )
    recv, inner_grid, hot_grid = kernel(
        decode_first_kernel,
        "decode_first",
        (grid_state, dec_send.T, edge_weights, node_weights, r_far),
        [((128, width), F32), ((128, width), F32), ((384, 192), BF)],
        [pltpu.VMEM((8, 128), F32)],
        products=1000,
        spaces=[VMEM] * 4 + [ANY],
    )
    band_two, mesh_two = kernel(
        process_kernel,
        "process",
        (acc, r1, r2, send_pair, packed, inner_one, hot, edge_weights, node_weights, recv),
        [((64, width), BF), ((16, width), BF)],
        products=8000,
        spaces=[VMEM] * 9 + [ANY],
    )
    with jax.named_scope("two_sides"):
        pair_two, cross_two = sides(band_two, band_two)
    (grid_out,) = kernel(
        decode_kernel,
        "decode",
        (grid_state, band_two, pair_two, cross_two, recv, inner_grid, hot_grid, edge_weights, node_weights),
        [((128, width), BF)],
        products=8000,
    )
    return (grid_out, mesh_two)


def solution(mesh):
    rows = P(("band", "lon"), None)
    in_specs = (rows, rows, P(), P(), rows, rows, rows, rows)
    return jax.shard_map(
        per_device, mesh=mesh, in_specs=in_specs, out_specs=(rows, rows), check_vma=False
    )
```

```python
import jax
import jax.numpy as jnp
from jax import lax
from jax.experimental import pallas as pl
from jax.experimental.pallas import tpu as pltpu
from jax.sharding import PartitionSpec as P

BF = jnp.bfloat16
F32 = jnp.float32
NONE = 384


def mm(a, b):
    return jnp.dot(a, b, preferred_element_type=F32)


def silu_of_half(half):
    return half + half * jnp.tanh(half)


def layer_norm(values):
    average = jnp.mean(values, axis=-1, keepdims=True)
    centred = values - average
    spread = jnp.mean(centred * centred, axis=-1, keepdims=True)
    return centred * lax.rsqrt(spread + 1e-05)


def update(state, inner, aggregate, w1, w2):
    inner = inner + mm(aggregate.astype(BF), w1)
    outer = layer_norm(mm(silu_of_half(0.5 * inner).astype(BF), w2))
    return (state.astype(F32) + outer).astype(BF)


def slot_of(target_band, band):
    step = jnp.where(band % 2 == 0, target_band - band, band - target_band)
    return jnp.where(step < 0, 2, step)


def one_hot(index, rows, dtype=BF):
    lanes = lax.broadcasted_iota(jnp.int32, (index.shape[0], rows), 1)
    return jnp.where(lanes == index, 1.0, 0.0).astype(dtype)


def pack_kernel(grid_ref, mesh_ref, enc_ref, proc_ref, far_ref, out_ref, enc_buf, proc_buf, far_buf, rows, sems):
    small = [
        pltpu.make_async_copy(src, dst, sems.at[n])
        for n, (src, dst) in enumerate(((enc_ref, enc_buf), (proc_ref, proc_buf), (far_ref, far_buf)))
    ]
    large = []
    large.append(pltpu.make_async_copy(grid_ref, out_ref.at[0:128], sems.at[3]))
    large.append(pltpu.make_async_copy(mesh_ref, out_ref.at[128:144], sems.at[4]))
    for copy in small + large:
        copy.start()
    band = lax.axis_index("band")
    rows[...] = jnp.full(rows.shape, float(NONE), F32)
    for copy in small:
        copy.wait()
    enc = enc_buf[...]
    rows[0:2, :] = (slot_of(enc >> 6, band) * 64 + (enc & 63)).astype(F32)
    proc = proc_buf[...]
    rows[2:8, 0:16] = (slot_of(proc >> 6, band) * 64 + (proc & 63)).astype(F32)
    far = far_buf[...]
    rows[8:9, 0:6] = (slot_of(far >> 2, band) * 64 + (far & 3) * 16).astype(F32)
    index = rows[...].astype(BF)
    out_ref[176:192, 0:128] = index
    out_ref[176:192, 128:512] = jnp.zeros((16, 384), BF)
    for copy in large:
        copy.wait()


def window(all_ref):
    return jnp.concatenate(
        [all_ref[l, 128 + 16 * s : 144 + 16 * s] for s in range(3) for l in range(4)], axis=0
    )


def encode_first(all_ref, ew_ref, sent_ref, hot_ref, spread_ref):
    rows_id = lax.broadcasted_iota(jnp.int32, (192, 128), 0)
    grid_rows = jnp.concatenate([all_ref[l, 0:128] for l in range(4)], axis=0)
    sent_ref[...] = 0.5 * mm(grid_rows, ew_ref[0, 0])
    for l in range(4):
        index = all_ref[l, 176:192, 0:128].astype(F32)
        cols = index.T.astype(jnp.int32)
        flat = index.astype(jnp.int32)
        for k in range(2):
            start = l * 256 + k * 128
            spread_ref[:, start : start + 128] = jnp.where(rows_id == flat[k : k + 1, :], 1.0, 0.0).astype(BF)
            hot_ref[start : start + 128] = one_hot(cols[:, k : k + 1], 192)


def encode_kernel(all_ref, ew_ref, acc_ref, p1_ref, far_ref, p2_ref, msgs, sent_ref, hot_ref, spread_ref):
    encode_first(all_ref, ew_ref, sent_ref, hot_ref, spread_ref)
    table = window(all_ref)
    recv = (0.5 * mm(table, ew_ref[0, 1])).astype(BF)
    for n in range(2):
        sent = [sent_ref[l * 128 : (l + 1) * 128] for l in (2 * n, 2 * n, 2 * n + 1, 2 * n + 1)]
        before = mm(hot_ref[n * 512 : (n + 1) * 512], recv) + jnp.concatenate(sent, axis=0)
        result = layer_norm(mm(silu_of_half(before).astype(BF), ew_ref[0, 2]))
        msgs[n * 512 : (n + 1) * 512] = result.astype(BF)
    total = mm(spread_ref[...], msgs[...])
    acc_ref[...] = total
    p1_ref[...] = total[0:128].astype(BF)
    cross = total[128:192].astype(BF)
    far_ref[...] = cross
    p2_ref[0:64] = cross
    p2_ref[64:128] = cross


def process_first_kernel(all_ref, acc_ref, r1_ref, far_ref, ew_ref, nw_ref, inner_ref, send_ref, hots):
    near_id = lax.broadcasted_iota(jnp.int32, (16, 1), 0)
    lanes = lax.broadcasted_iota(jnp.int32, (16, 256), 1)
    far = []
    for l in range(4):
        cols = all_ref[l, 176:192, 0:128].astype(F32).T.astype(jnp.int32)
        for k in range(6):
            hit = jnp.logical_or(lanes == cols[0:16, 2 + k : 3 + k], lanes == near_id + (192 + 16 * l))
            hots[l * 96 + 16 * k : l * 96 + 16 * k + 16] = jnp.where(hit, 1.0, 0.0).astype(BF)
        far.append(jnp.logical_or(lanes[0:8] == cols[0:8, 8:9], lanes[0:8] == 192 + 16 * l))
    hots[384:416] = jnp.concatenate([jnp.where(hit, 1.0, 0.0) for hit in far], axis=0).astype(BF)
    table = window(all_ref)
    inner = mm(table, nw_ref[0, 0])
    inner_ref[...] = jnp.concatenate([inner[0:64], inner[128:192]], axis=0)
    sums = acc_ref[64:128] + r1_ref[0:64].astype(F32) + far_ref[...].astype(F32)
    one = update(table[64:128], inner[64:128], sums, nw_ref[0, 1], nw_ref[0, 2])
    send_ref[...] = (0.5 * mm(one, ew_ref[1, 0])).astype(BF)


def process_kernel(
    acc_ref, r1_ref, r2_ref, send_ref, all_ref, inner_ref, hots, ew_ref, nw_ref, after_ref, band_ref, own_ref
):
    table = window(all_ref)
    table = jnp.concatenate([table[0:64], table[128:192]], axis=0)
    own = acc_ref[0:64] + r1_ref[64:128].astype(F32) + r2_ref[0:64].astype(F32)
    cross = acc_ref[128:192] + r2_ref[64:128].astype(F32)
    sums = jnp.concatenate([own, cross], axis=0)
    one = update(table, inner_ref[...], sums, nw_ref[0, 1], nw_ref[0, 2])
    send = (0.5 * mm(one, ew_ref[1, 0])).astype(BF)
    recv = (0.5 * mm(one[0:64], ew_ref[1, 1])).astype(BF)
    both = jnp.concatenate([send[0:64], send_ref[...], send[64:128], recv], axis=0)
    inner = mm(one[0:64], nw_ref[1, 0])
    near_id = lax.broadcasted_iota(jnp.int32, (16, 1), 0)
    far_id = lax.broadcasted_iota(jnp.int32, (8, 1), 0)
    near, far = [], []
    before = mm(hots[...], both)
    messages = layer_norm(mm(silu_of_half(before).astype(BF), ew_ref[1, 2]))
    for l in range(4):
        total = messages[96 * l : 96 * l + 16]
        for k in range(1, 6):
            total = total + messages[96 * l + 16 * k : 96 * l + 16 * k + 16]
        near.append(total)
    for l in range(4):
        values = jnp.where(far_id < 6, messages[384 + 8 * l : 392 + 8 * l], 0.0)
        far.append(jnp.sum(values, axis=0, keepdims=True))
    parts = [a + jnp.where(near_id == 0, b, 0.0) for a, b in zip(near, far)]
    sums = jnp.concatenate(parts, axis=0)
    two = update(one[0:64], inner, sums, nw_ref[1, 1], nw_ref[1, 2])
    band_ref[...] = two
    lon = lax.axis_index("lon")
    for l in range(4):

        @pl.when(lon == l)
        def _():
            own_ref[...] = two[16 * l : 16 * l + 16]


def decode_first_kernel(grid_ref, dec_ref, ew_ref, nw_ref, after_ref, recv_ref, inner_ref, hots, rows):
    index = dec_ref[...]
    rows[...] = jnp.zeros(rows.shape, F32)
    rows[0:3, :] = (slot_of(index >> 6, lax.axis_index("band")) * 64 + (index & 63)).astype(F32)
    index = rows[...].T.astype(jnp.int32)
    for k in range(3):
        hots[k * 128 : (k + 1) * 128] = one_hot(index[:, k : k + 1], 192)
    recv_ref[...] = 0.5 * mm(grid_ref[...], ew_ref[2, 1])
    inner_ref[...] = mm(grid_ref[...], nw_ref[2, 0])


def decode_kernel(grid_ref, own_ref, pair_ref, cross_ref, recv_ref, inner_ref, hots, ew_ref, nw_ref, out_ref):
    table = jnp.concatenate([own_ref[...], pair_ref[...], cross_ref[...]], axis=0)
    send = (0.5 * mm(table, ew_ref[2, 0])).astype(BF)
    recv = recv_ref[...]
    before = mm(hots[...], send) + jnp.concatenate([recv, recv, recv], axis=0)
    messages = layer_norm(mm(silu_of_half(before).astype(BF), ew_ref[2, 2]))
    sums = messages[0:128] + messages[128:256] + messages[256:384]
    out_ref[...] = update(grid_ref[...], inner_ref[...], sums, nw_ref[2, 1], nw_ref[2, 2])


VMEM = pl.BlockSpec(memory_space=pltpu.VMEM)
HBM = pl.BlockSpec(memory_space=pltpu.HBM)
ANY = pl.BlockSpec(memory_space=pl.ANY)
MIB = 1024 * 1024


def kernel(body, name, operands, outs, scratch=(), limit=16, products=4000, spaces=None):
    return pl.pallas_call(
        body,
        in_specs=spaces or [VMEM] * len(operands),
        out_specs=[VMEM] * len(outs),
        out_shape=[jax.ShapeDtypeStruct(dims, kind) for dims, kind in outs],
        scratch_shapes=list(scratch),
        compiler_params=pltpu.CompilerParams(vmem_limit_bytes=limit * MIB),
        cost_estimate=pl.CostEstimate(
            flops=2 * products * 512 * 512, bytes_accessed=8 * MIB, transcendentals=0
        ),
        name=name,
    )(*operands)


def per_device(
    grid_state, mesh_state, edge_weights, node_weights, enc_recv, proc_send, long_send, dec_send
):
    width = grid_state.shape[1]
    bands = lax.axis_size("band")
    across = [(i, i + 1 if i % 2 else i - 1) for i in range(1, bands - 1)]
    within = [(i, i ^ 1) for i in range(bands)]
    beyond = [(i, i + 2) for i in range(1, bands - 2, 2)]
    beyond += [(i, i - 2) for i in range(2, bands, 2)]

    def sides(pair_block, cross_block):
        cross = lax.ppermute(cross_block, "band", across)
        pair = lax.ppermute(pair_block, "band", within)
        return pair, cross

    small = pltpu.SemaphoreType.DMA((5,)), pltpu.VMEM((16, 128), F32)
    inputs = (grid_state, mesh_state, enc_recv.T, proc_send.T, long_send)
    inputs = [pltpu.with_memory_space_constraint(x, pltpu.HBM) for x in inputs]
    buffers = [pltpu.VMEM(x.shape, jnp.int32) for x in inputs[2:]]
    (packed,) = kernel(
        pack_kernel,
        "pack",
        inputs,
        [((192, width), BF)],
        [*buffers, small[1], small[0]],
        products=8000,
        spaces=[HBM] * 5,
    )
    with jax.named_scope("mesh_sides"):
        pair_state, cross_state = sides(mesh_state, mesh_state)
        packed = packed.at[144:176].set(jnp.concatenate([pair_state, cross_state], axis=0))
    with jax.named_scope("gather_lon"):
        packed = lax.all_gather(packed, "lon", axis=0)
    acc, p1, far, p2 = kernel(
        encode_kernel,
        "encode",
        (packed, edge_weights),
        [((192, width), F32), ((128, width), BF), ((64, width), BF), ((128, width), BF)],
        [
            pltpu.VMEM((1024, width), BF),
            pltpu.VMEM((512, width), F32),
            pltpu.VMEM((1024, 192), BF),
            pltpu.VMEM((192, 1024), BF),
        ],
        products=8000,
    )
    with jax.named_scope("sum_pair"):
        r1 = lax.ppermute(p1, "band", within)
        r_far = lax.ppermute(far, "band", beyond)
    with jax.named_scope("sum_cross"):
        chip = acc[0:64] + r1[64:128].astype(F32)
        r2 = lax.ppermute(p2.at[64:128].set(chip.astype(BF)), "band", across)
    inner_one, send_pair, hot = kernel(
        process_first_kernel,
        "process_first",
        (packed, acc, r1, r_far, edge_weights, node_weights),
        [((128, width), F32), ((64, width), BF), ((416, 256), BF)],
        products=1000,
    )
    recv, inner_grid, hot_grid = kernel(
        decode_first_kernel,
        "decode_first",
        (grid_state, dec_send.T, edge_weights, node_weights, r_far),
        [((128, width), F32), ((128, width), F32), ((384, 192), BF)],
        [pltpu.VMEM((8, 128), F32)],
        products=1000,
        spaces=[VMEM] * 4 + [ANY],
    )
    band_two, mesh_two = kernel(
        process_kernel,
        "process",
        (acc, r1, r2, send_pair, packed, inner_one, hot, edge_weights, node_weights, recv),
        [((64, width), BF), ((16, width), BF)],
        products=8000,
        spaces=[VMEM] * 9 + [ANY],
    )
    with jax.named_scope("two_sides"):
        pair_two, cross_two = sides(band_two, band_two)
    (grid_out,) = kernel(
        decode_kernel,
        "decode",
        (grid_state, band_two, pair_two, cross_two, recv, inner_grid, hot_grid, edge_weights, node_weights),
        [((128, width), BF)],
        products=8000,
    )
    return (grid_out, mesh_two)


def solution(mesh):
    rows = P(("band", "lon"), None)
    in_specs = (rows, rows, P(), P(), rows, rows, rows, rows)
    return jax.shard_map(
        per_device, mesh=mesh, in_specs=in_specs, out_specs=(rows, rows), check_vma=False
    )
```

```python
import jax
import jax.numpy as jnp
from jax import lax
from jax.experimental import pallas as pl
from jax.experimental.pallas import tpu as pltpu
from jax.sharding import PartitionSpec as P

BF = jnp.bfloat16
F32 = jnp.float32
NONE = 384


def mm(a, b):
    return jnp.dot(a, b, preferred_element_type=F32)


def silu_of_half(half):
    return half + half * jnp.tanh(half)


def layer_norm(values):
    average = jnp.mean(values, axis=-1, keepdims=True)
    centred = values - average
    spread = jnp.mean(centred * centred, axis=-1, keepdims=True)
    return centred * lax.rsqrt(spread + 1e-05)


def update(state, inner, aggregate, w1, w2):
    inner = inner + mm(aggregate.astype(BF), w1)
    outer = layer_norm(mm(silu_of_half(0.5 * inner).astype(BF), w2))
    return (state.astype(F32) + outer).astype(BF)


def slot_of(target_band, band):
    step = jnp.where(band % 2 == 0, target_band - band, band - target_band)
    return jnp.where(step < 0, 2, step)


def one_hot(index, rows, dtype=BF):
    lanes = lax.broadcasted_iota(jnp.int32, (index.shape[0], rows), 1)
    return jnp.where(lanes == index, 1.0, 0.0).astype(dtype)


def pack_kernel(grid_ref, mesh_ref, enc_ref, proc_ref, far_ref, out_ref, enc_buf, proc_buf, far_buf, rows, sems):
    small = [
        pltpu.make_async_copy(src, dst, sems.at[n])
        for n, (src, dst) in enumerate(((enc_ref, enc_buf), (proc_ref, proc_buf), (far_ref, far_buf)))
    ]
    large = []
    large.append(pltpu.make_async_copy(grid_ref, out_ref.at[0:128], sems.at[3]))
    large.append(pltpu.make_async_copy(mesh_ref, out_ref.at[128:144], sems.at[4]))
    for copy in small + large:
        copy.start()
    band = lax.axis_index("band")
    rows[...] = jnp.full(rows.shape, float(NONE), F32)
    for copy in small:
        copy.wait()
    enc = enc_buf[...]
    rows[0:2, :] = (slot_of(enc >> 6, band) * 64 + (enc & 63)).astype(F32)
    proc = proc_buf[...]
    rows[2:8, 0:16] = (slot_of(proc >> 6, band) * 64 + (proc & 63)).astype(F32)
    far = far_buf[...]
    rows[8:9, 0:6] = (slot_of(far >> 2, band) * 64 + (far & 3) * 16).astype(F32)
    index = rows[...].astype(BF)
    out_ref[176:192, 0:128] = index
    out_ref[176:192, 128:512] = jnp.zeros((16, 384), BF)
    for copy in large:
        copy.wait()


def window(all_ref):
    return jnp.concatenate(
        [all_ref[l, 128 + 16 * s : 144 + 16 * s] for s in range(3) for l in range(4)], axis=0
    )


def encode_first(all_ref, hot_ref, spread_ref):
    rows_id = lax.broadcasted_iota(jnp.int32, (192, 128), 0)
    for l in range(4):
        index = all_ref[l, 176:192, 0:128].astype(F32)
        cols = index.T.astype(jnp.int32)
        flat = index.astype(jnp.int32)
        for k in range(2):
            start = l * 256 + k * 128
            spread_ref[:, start : start + 128] = jnp.where(rows_id == flat[k : k + 1, :], 1.0, 0.0).astype(BF)
            hot_ref[start : start + 128] = one_hot(cols[:, k : k + 1], 192)


def encode_kernel(all_ref, ew_ref, acc_ref, p1_ref, far_ref, p2_ref, msgs, hot_ref, spread_ref):
    encode_first(all_ref, hot_ref, spread_ref)
    table = window(all_ref)
    recv = (0.5 * mm(table, ew_ref[0, 1])).astype(BF)
    for n in range(2):
        grid_rows = jnp.concatenate([all_ref[2 * n, 0:128], all_ref[2 * n + 1, 0:128]], axis=0)
        sent = 0.5 * mm(grid_rows, ew_ref[0, 0])
        sent = [sent[0:128], sent[0:128], sent[128:256], sent[128:256]]
        before = mm(hot_ref[n * 512 : (n + 1) * 512], recv) + jnp.concatenate(sent, axis=0)
        result = layer_norm(mm(silu_of_half(before).astype(BF), ew_ref[0, 2]))
        msgs[n * 512 : (n + 1) * 512] = result.astype(BF)
    total = mm(spread_ref[...], msgs[...])
    acc_ref[...] = total
    p1_ref[...] = total[0:128].astype(BF)
    cross = total[128:192].astype(BF)
    far_ref[...] = cross
    p2_ref[0:64] = cross
    p2_ref[64:128] = cross


def process_first_kernel(all_ref, acc_ref, r1_ref, far_ref, ew_ref, nw_ref, inner_ref, send_ref, hots):
    near_id = lax.broadcasted_iota(jnp.int32, (16, 1), 0)
    lanes = lax.broadcasted_iota(jnp.int32, (16, 256), 1)
    far = []
    for l in range(4):
        cols = all_ref[l, 176:192, 0:128].astype(F32).T.astype(jnp.int32)
        for k in range(6):
            hit = jnp.logical_or(lanes == cols[0:16, 2 + k : 3 + k], lanes == near_id + (192 + 16 * l))
            hots[l * 96 + 16 * k : l * 96 + 16 * k + 16] = jnp.where(hit, 1.0, 0.0).astype(BF)
        far.append(jnp.logical_or(lanes[0:8] == cols[0:8, 8:9], lanes[0:8] == 192 + 16 * l))
    hots[384:416] = jnp.concatenate([jnp.where(hit, 1.0, 0.0) for hit in far], axis=0).astype(BF)
    table = window(all_ref)
    inner = mm(table, nw_ref[0, 0])
    inner_ref[...] = jnp.concatenate([inner[0:64], inner[128:192]], axis=0)
    sums = acc_ref[64:128] + r1_ref[0:64].astype(F32) + far_ref[...].astype(F32)
    one = update(table[64:128], inner[64:128], sums, nw_ref[0, 1], nw_ref[0, 2])
    send_ref[...] = (0.5 * mm(one, ew_ref[1, 0])).astype(BF)


def process_kernel(
    acc_ref, r1_ref, r2_ref, send_ref, all_ref, inner_ref, hots, ew_ref, nw_ref, after_ref, band_ref, own_ref
):
    table = window(all_ref)
    table = jnp.concatenate([table[0:64], table[128:192]], axis=0)
    own = acc_ref[0:64] + r1_ref[64:128].astype(F32) + r2_ref[0:64].astype(F32)
    cross = acc_ref[128:192] + r2_ref[64:128].astype(F32)
    sums = jnp.concatenate([own, cross], axis=0)
    one = update(table, inner_ref[...], sums, nw_ref[0, 1], nw_ref[0, 2])
    send = (0.5 * mm(one, ew_ref[1, 0])).astype(BF)
    recv = (0.5 * mm(one[0:64], ew_ref[1, 1])).astype(BF)
    both = jnp.concatenate([send[0:64], send_ref[...], send[64:128], recv], axis=0)
    inner = mm(one[0:64], nw_ref[1, 0])
    near_id = lax.broadcasted_iota(jnp.int32, (16, 1), 0)
    far_id = lax.broadcasted_iota(jnp.int32, (8, 1), 0)
    near, far = [], []
    before = mm(hots[...], both)
    messages = layer_norm(mm(silu_of_half(before).astype(BF), ew_ref[1, 2]))
    for l in range(4):
        total = messages[96 * l : 96 * l + 16]
        for k in range(1, 6):
            total = total + messages[96 * l + 16 * k : 96 * l + 16 * k + 16]
        near.append(total)
    for l in range(4):
        values = jnp.where(far_id < 6, messages[384 + 8 * l : 392 + 8 * l], 0.0)
        far.append(jnp.sum(values, axis=0, keepdims=True))
    parts = [a + jnp.where(near_id == 0, b, 0.0) for a, b in zip(near, far)]
    sums = jnp.concatenate(parts, axis=0)
    two = update(one[0:64], inner, sums, nw_ref[1, 1], nw_ref[1, 2])
    band_ref[...] = two
    lon = lax.axis_index("lon")
    for l in range(4):

        @pl.when(lon == l)
        def _():
            own_ref[...] = two[16 * l : 16 * l + 16]


def decode_first_kernel(grid_ref, dec_ref, ew_ref, nw_ref, after_ref, recv_ref, inner_ref, hots, rows):
    index = dec_ref[...]
    rows[...] = jnp.zeros(rows.shape, F32)
    rows[0:3, :] = (slot_of(index >> 6, lax.axis_index("band")) * 64 + (index & 63)).astype(F32)
    index = rows[...].T.astype(jnp.int32)
    for k in range(3):
        hots[k * 128 : (k + 1) * 128] = one_hot(index[:, k : k + 1], 192)
    recv_ref[...] = 0.5 * mm(grid_ref[...], ew_ref[2, 1])
    inner_ref[...] = mm(grid_ref[...], nw_ref[2, 0])


def decode_kernel(grid_ref, own_ref, pair_ref, cross_ref, recv_ref, inner_ref, hots, ew_ref, nw_ref, out_ref):
    table = jnp.concatenate([own_ref[...], pair_ref[...], cross_ref[...]], axis=0)
    send = (0.5 * mm(table, ew_ref[2, 0])).astype(BF)
    recv = recv_ref[...]
    before = mm(hots[...], send) + jnp.concatenate([recv, recv, recv], axis=0)
    messages = layer_norm(mm(silu_of_half(before).astype(BF), ew_ref[2, 2]))
    sums = messages[0:128] + messages[128:256] + messages[256:384]
    out_ref[...] = update(grid_ref[...], inner_ref[...], sums, nw_ref[2, 1], nw_ref[2, 2])


VMEM = pl.BlockSpec(memory_space=pltpu.VMEM)
HBM = pl.BlockSpec(memory_space=pltpu.HBM)
ANY = pl.BlockSpec(memory_space=pl.ANY)
MIB = 1024 * 1024


def kernel(body, name, operands, outs, scratch=(), limit=16, products=4000, spaces=None):
    return pl.pallas_call(
        body,
        in_specs=spaces or [VMEM] * len(operands),
        out_specs=[VMEM] * len(outs),
        out_shape=[jax.ShapeDtypeStruct(dims, kind) for dims, kind in outs],
        scratch_shapes=list(scratch),
        compiler_params=pltpu.CompilerParams(vmem_limit_bytes=limit * MIB),
        cost_estimate=pl.CostEstimate(
            flops=2 * products * 512 * 512, bytes_accessed=8 * MIB, transcendentals=0
        ),
        name=name,
    )(*operands)


def per_device(
    grid_state, mesh_state, edge_weights, node_weights, enc_recv, proc_send, long_send, dec_send
):
    width = grid_state.shape[1]
    bands = lax.axis_size("band")
    across = [(i, i + 1 if i % 2 else i - 1) for i in range(1, bands - 1)]
    within = [(i, i ^ 1) for i in range(bands)]
    beyond = [(i, i + 2) for i in range(1, bands - 2, 2)]
    beyond += [(i, i - 2) for i in range(2, bands, 2)]

    def sides(pair_block, cross_block):
        cross = lax.ppermute(cross_block, "band", across)
        pair = lax.ppermute(pair_block, "band", within)
        return pair, cross

    small = pltpu.SemaphoreType.DMA((5,)), pltpu.VMEM((16, 128), F32)
    inputs = (grid_state, mesh_state, enc_recv.T, proc_send.T, long_send)
    inputs = [pltpu.with_memory_space_constraint(x, pltpu.HBM) for x in inputs]
    buffers = [pltpu.VMEM(x.shape, jnp.int32) for x in inputs[2:]]
    (packed,) = kernel(
        pack_kernel,
        "pack",
        inputs,
        [((192, width), BF)],
        [*buffers, small[1], small[0]],
        products=8000,
        spaces=[HBM] * 5,
    )
    with jax.named_scope("mesh_sides"):
        pair_state, cross_state = sides(mesh_state, mesh_state)
        packed = packed.at[144:176].set(jnp.concatenate([pair_state, cross_state], axis=0))
    with jax.named_scope("gather_lon"):
        packed = lax.all_gather(packed, "lon", axis=0)
    acc, p1, far, p2 = kernel(
        encode_kernel,
        "encode",
        (packed, edge_weights),
        [((192, width), F32), ((128, width), BF), ((64, width), BF), ((128, width), BF)],
        [
            pltpu.VMEM((1024, width), BF),
            pltpu.VMEM((1024, 192), BF),
            pltpu.VMEM((192, 1024), BF),
        ],
        products=8000,
    )
    with jax.named_scope("sum_pair"):
        r1 = lax.ppermute(p1, "band", within)
        r_far = lax.ppermute(far, "band", beyond)
    with jax.named_scope("sum_cross"):
        chip = acc[0:64] + r1[64:128].astype(F32)
        r2 = lax.ppermute(p2.at[64:128].set(chip.astype(BF)), "band", across)
    inner_one, send_pair, hot = kernel(
        process_first_kernel,
        "process_first",
        (packed, acc, r1, r_far, edge_weights, node_weights),
        [((128, width), F32), ((64, width), BF), ((416, 256), BF)],
        products=1000,
    )
    recv, inner_grid, hot_grid = kernel(
        decode_first_kernel,
        "decode_first",
        (grid_state, dec_send.T, edge_weights, node_weights, r_far),
        [((128, width), F32), ((128, width), F32), ((384, 192), BF)],
        [pltpu.VMEM((8, 128), F32)],
        products=1000,
        spaces=[VMEM] * 4 + [ANY],
    )
    band_two, mesh_two = kernel(
        process_kernel,
        "process",
        (acc, r1, r2, send_pair, packed, inner_one, hot, edge_weights, node_weights, recv),
        [((64, width), BF), ((16, width), BF)],
        products=8000,
        spaces=[VMEM] * 9 + [ANY],
    )
    with jax.named_scope("two_sides"):
        pair_two, cross_two = sides(band_two, band_two)
    (grid_out,) = kernel(
        decode_kernel,
        "decode",
        (grid_state, band_two, pair_two, cross_two, recv, inner_grid, hot_grid, edge_weights, node_weights),
        [((128, width), BF)],
        products=8000,
    )
    return (grid_out, mesh_two)


def solution(mesh):
    rows = P(("band", "lon"), None)
    in_specs = (rows, rows, P(), P(), rows, rows, rows, rows)
    return jax.shard_map(
        per_device, mesh=mesh, in_specs=in_specs, out_specs=(rows, rows), check_vma=False
    )
```
